128 devices in a mesh: dp: 16 (over y, x), samp: 4 (over z_lo, core), col: 2 (over z_hi).
Axes of the slice: x: 4, y: 4, z: 4 (z_hi: 2, z_lo: 2; z = z_hi * 2 + z_lo), core: 2. Of those that a mesh axis runs over, the one named last changes fastest.
Arguments:
- looked_rows: bfloat16 [64, 1920, 128], P(('dp', 'samp'), None, 'col'), may hold values from -6 to 6
- bag_ids: int32 [64, 1920], P(('dp', 'samp')), may hold values from 0 to 959, never falling along the last dimension, each value on 1 to 4 neighbouring positions
- slot_of: int32 [40], replicated, may hold values from 0 to 39, each once
- labels: int32 [1536], P(('dp', 'samp')), may hold values 0 or 1
- out_weight: bfloat16 [3, 128], replicated, may hold values from -0.02734375 to 0.02734375
- filter_first: bfloat16 [128, 1521], replicated, may hold values from -0.15625 to 0.15625
- filter_second: bfloat16 [128, 4992], replicated, may hold values from -0.078125 to 0.078125
- filter_third: bfloat16 [128, 4992], replicated, may hold values from -0.078125 to 0.078125
Outputs:
- row_grads: bfloat16 [64, 1920, 128], P(('dp', 'samp'), None, 'col')
- grad_first: float32 [128, 1521], P('dp')
- grad_second: float32 [128, 4992], P('dp')
- grad_third: float32 [128, 4992], P('dp')
The draws below stay inside these ranges and needn't reach their ends.
Inputs may be any that keep to these rules, and one draw needn't show every extreme that they name: `bag_ids`: within each owner's row, bag numbers never fall; each of the 960 bags has 1 to 4 entries and some bag exactly 4. `slot_of`: each slot number once.
All inputs are finite; a program needn't handle non-finite values. No bound on the sum of `labels` on one device may be relied on, other than what follows from the above.
Results may differ from the reference program's by a relative error of at most 0.014.
Values may be sent and summed in bfloat16 or wider, within the bound.
A program may use at most 64 MiB of HBM per device.

```python
import math
import jax
import jax.numpy as jnp
import numpy as np
from jax import lax

D = 128
FIELDS = 39
H = 128
SLOTS = 40
MOST_BAG = 4
SAMP_DEV = 24
ENTRIES = 1920
TOTAL = 1536
N_DP = 16
N_SAMP = 4


def with_ends(array, rng, least, top_value):
    longest = array.shape.index(max(array.shape))
    spots = []
    for shift in (0, 1):
        where = [jax.random.randint(jax.random.fold_in(rng, axis), (), 0, length) for axis, length in enumerate(array.shape)]
        where[longest] = (where[longest] + shift) % array.shape[longest]
        spots.append(tuple(where))
    return array.at[spots[0]].set(least).at[spots[1]].set(top_value)


def level_of(own_key, extent, shards, low, largest):
    def one(dim, blocks):
        draws = jax.random.uniform(jax.random.fold_in(jax.random.fold_in(own_key, 6), dim), (blocks,), jnp.float32, low / len(shards), largest / len(shards))
        return jnp.repeat(jnp.exp(draws), extent[dim] // blocks).reshape((-1,) + (1,) * (len(extent) - dim - 1))

    level = one(*shards[0])
    for cut in shards[1:]:
        level = level * one(*cut)
    return level


def length_profile(count, total, bound, skew):
    loads = [(1 << 20) // math.isqrt(grade ** skew) + 1 for grade in range(2, count + 1)]
    rest, holding = total - bound - (count - 1), [1] * (count - 1)
    while rest > 0:
        movable = [i for i in range(count - 1) if holding[i] < bound]
        mass, left = sum([loads[i] for i in movable]), rest
        for i in movable:
            more = min(bound - holding[i], max(1, left * loads[i] // mass), rest)
            holding[i] = holding[i] + more
            rest = rest - more
    return np.array([bound] + holding)


def uneven_parts(rng, number_of, total, limit, skew):
    if number_of == 2:
        one = jax.random.randint(rng, (), max(1, total - limit), min(limit, total - 1) + 1)
        return jnp.stack([one, total - one])
    tallies = jnp.asarray(length_profile(number_of, total, limit, skew), jnp.int32)
    couples = (number_of - 1) // 2
    source_of, receiver = tallies[1:1 + 2 * couples:2], tallies[2:2 + 2 * couples:2]
    room = jnp.minimum(source_of - 1, limit - receiver)
    passed = jax.random.randint(jax.random.fold_in(rng, 1), (couples,), 0, 1 << 20) % (room + 1)
    tallies = tallies.at[1:1 + 2 * couples:2].set(source_of - passed).at[2:2 + 2 * couples:2].set(receiver + passed)
    return tallies[jax.random.permutation(jax.random.fold_in(rng, 2), number_of)]


def scatter_about(rng, shape, scale, most, split=(), held_as=jnp.bfloat16):
    array = scale * jax.random.normal(rng, shape, jnp.float32)
    if split:
        array = array * level_of(rng, shape, split, -0.22, 0.18)
    return jnp.clip(array, -most, most).astype(held_as)


def setup_inputs(seed: int = 0) -> dict:
    seeds = jax.random.split(jax.random.key(seed), 9)
    return {
        "looked_rows": scatter_about(seeds[0], (N_DP * N_SAMP, ENTRIES, D), 0.8, 6.0, ((0, 64), (2, 2))),
        "bag_ids": jax.vmap(lambda own: jnp.searchsorted(jnp.cumsum(uneven_parts(own, SAMP_DEV * SLOTS, ENTRIES, MOST_BAG, 2)), jnp.arange(ENTRIES), side="right"))(jax.random.split(seeds[1], (N_DP * N_SAMP))).reshape((N_DP * N_SAMP, ENTRIES)).astype(jnp.int32),
        "slot_of": jax.random.permutation(seeds[2], SLOTS).astype(jnp.int32),
        "labels": with_ends((jax.random.randint(seeds[3], (TOTAL,), 0, 3) < 1).astype(jnp.int32), jax.random.fold_in(seeds[3], 1), 0, 1),
        "out_weight": scatter_about(seeds[4], (3, H), (3 * H * D) ** -0.5, 0.02734375),
        "filter_first": scatter_about(seeds[5], (H, FIELDS * FIELDS), (FIELDS * FIELDS) ** -0.5, 0.15625),
        "filter_second": scatter_about(seeds[6], (H, H * FIELDS), (H * FIELDS) ** -0.5, 0.078125),
        "filter_third": scatter_about(seeds[7], (H, H * FIELDS), (H * FIELDS) ** -0.5, 0.078125),
    }


loss_scale = 16.0


def outer_block(previous, anchor):
    rows_here = previous.shape[0]
    spread_rows = previous.astype(jnp.float32)[:, :, None, :] * anchor.astype(jnp.float32)[:, None, :, :]
    rounded = spread_rows.astype(jnp.bfloat16).reshape(rows_here, previous.shape[1] * anchor.shape[1], anchor.shape[2])
    return lax.optimization_barrier(rounded).astype(jnp.float32)


def forward_layer(filter_weight, previous, anchor):
    outer_products = outer_block(previous, anchor)
    projected_maps = jnp.einsum("fn,vnx->vfx", filter_weight.astype(jnp.float32), outer_products, precision=lax.Precision.HIGHEST)
    return projected_maps.astype(jnp.bfloat16)


def backward_layer(filter_weight, cotangent, previous, anchor):
    outer_products = outer_block(previous, anchor)
    broad_cotangent = cotangent.astype(jnp.float32)
    weight_gradient = jnp.einsum("yhn,ymn->hm", broad_cotangent, outer_products, precision=lax.Precision.HIGHEST)
    spread_rows = jnp.einsum("gt,lgi->lti", filter_weight.astype(jnp.float32), broad_cotangent, precision=lax.Precision.HIGHEST)
    spread_rows = spread_rows.reshape(previous.shape[0], previous.shape[1], anchor.shape[1], anchor.shape[2])
    grad_previous = jnp.sum(spread_rows * anchor.astype(jnp.float32)[:, None, :, :], axis=2)
    grad_anchor = jnp.sum(spread_rows * previous.astype(jnp.float32)[:, :, None, :], axis=1)
    return weight_gradient, grad_previous, grad_anchor


def reference(looked_rows, bag_ids, slot_of, labels, out_weight, filter_first, filter_second, filter_third):
    slot_span = SLOTS // N_SAMP
    group_size = SAMP_DEV * N_SAMP
    bag_count = SAMP_DEV * SLOTS
    owners = N_DP * N_SAMP

    def pool_device(operands):
        rows_dev, ids_dev = operands
        member = (ids_dev[None, :] == jnp.arange(bag_count, dtype=jnp.int32)[:, None]).astype(jnp.float32)
        return jnp.dot(member, rows_dev.astype(jnp.float32), precision=lax.Precision.HIGHEST).astype(jnp.bfloat16)

    pooled = lax.map(pool_device, (looked_rows, bag_ids))
    pooled = pooled.reshape(N_DP, N_SAMP, group_size, slot_span, D).transpose(0, 2, 1, 3, 4)
    pooled = pooled.reshape(N_DP * group_size, SLOTS, D)
    field_slots = slot_of[:FIELDS].astype(jnp.int32)
    fields_all = jnp.take(pooled, field_slots, axis=1)
    field_blocks = fields_all.reshape(owners, SAMP_DEV, FIELDS, D)
    label_blocks = labels.reshape(owners, SAMP_DEV).astype(jnp.float32)
    weights_out = out_weight.astype(jnp.float32)

    def per_block(running, operands):
        anchor, targets = operands
        layer_one = forward_layer(filter_first, anchor, anchor)
        layer_two = forward_layer(filter_second, layer_one, anchor)
        layer_three = forward_layer(filter_third, layer_two, anchor)
        maps_one = jnp.sum(layer_one.astype(jnp.float32), axis=2)
        maps_two = jnp.sum(layer_two.astype(jnp.float32), axis=2)
        maps_three = jnp.sum(layer_three.astype(jnp.float32), axis=2)
        logits = jnp.dot(maps_one, weights_out[0], precision=lax.Precision.HIGHEST)
        logits = logits + jnp.dot(maps_two, weights_out[1], precision=lax.Precision.HIGHEST)
        logits = logits + jnp.dot(maps_three, weights_out[2], precision=lax.Precision.HIGHEST)
        residual_slope = loss_scale * (jax.nn.sigmoid(logits) - targets)
        direct_one = (residual_slope[:, None] * weights_out[0][None, :])[:, :, None]
        direct_two = (residual_slope[:, None] * weights_out[1][None, :])[:, :, None]
        direct_three = (residual_slope[:, None] * weights_out[2][None, :])[:, :, None]
        cotan_three = jnp.broadcast_to(direct_three, layer_three.shape).astype(jnp.bfloat16)
        grad_three, back_two, base_three = backward_layer(filter_third, cotan_three, layer_two, anchor)
        cotan_two = (direct_two + back_two).astype(jnp.bfloat16)
        grad_two, back_one, base_two = backward_layer(filter_second, cotan_two, layer_one, anchor)
        cotan_one = (direct_one + back_one).astype(jnp.bfloat16)
        grad_one, back_zero, base_one = backward_layer(filter_first, cotan_one, anchor, anchor)
        grad_fields = (back_zero + base_one + base_two + base_three).astype(jnp.bfloat16)
        return (running[0] + grad_one, running[1] + grad_two, running[2] + grad_three), grad_fields

    starting = (jnp.zeros((H, FIELDS * FIELDS), jnp.float32), jnp.zeros((H, H * FIELDS), jnp.float32), jnp.zeros((H, H * FIELDS), jnp.float32))
    totals, grad_blocks = lax.scan(per_block, starting, (field_blocks, label_blocks))
    grad_fields = grad_blocks.reshape(N_DP * group_size, FIELDS, D)
    slot_grads = jnp.zeros((N_DP * group_size, SLOTS, D), jnp.bfloat16).at[:, field_slots].set(grad_fields)
    bag_grads = slot_grads.reshape(N_DP, group_size, N_SAMP, slot_span, D).transpose(0, 2, 1, 3, 4)
    bag_grads = bag_grads.reshape(owners, bag_count, D)
    row_grads = jnp.take_along_axis(bag_grads, bag_ids.astype(jnp.int32)[:, :, None], axis=1)
    return row_grads, totals[0], totals[1], totals[2]
```

```python
import functools

import jax
import jax.numpy as jnp
from jax import lax
from jax.experimental import pallas as pl
from jax.experimental.pallas import tpu as pltpu
from jax.sharding import PartitionSpec as P

F = 39
FP = 40
H = 128
HALF = 20
PAIRS = 848
PL = 896
LANES = 1536
T2N = 12
BAGS = 512
SCALE = 16.0
BF = jnp.bfloat16
F32 = jnp.float32
VMEM = pl.BlockSpec(memory_space=pltpu.VMEM)
SMEM = pl.BlockSpec(memory_space=pltpu.SMEM)


def dot(a, b, ca, cb):
    return lax.dot_general(a, b, (((ca,), (cb,)), ((), ())), preferred_element_type=F32)


def lane_columns(row):
    n = row.shape[1] // 128
    blocks = [
        jnp.transpose(jnp.broadcast_to(row[:, b * 128 : (b + 1) * 128], (128, 128)))
        for b in range(n)
    ]
    return jnp.concatenate(blocks, axis=0)


def bag_places(ids):
    tens = (ids * 6554) >> 16
    twenties = (ids * 3277) >> 16
    row = twenties * 10 + (ids - tens * 10)
    row = row + 8 * ((row * 8739) >> 20)
    return row, tens - 2 * twenties


def pool(ids, rows):
    place, half = bag_places(ids)
    half_col = lane_columns(half.astype(F32))
    lane = lax.broadcasted_iota(jnp.int32, half_col.shape, 1)
    keep = half_col == (lane >= 64).astype(F32)
    wide = jnp.concatenate([rows, rows], axis=1)
    wide = jnp.where(keep, wide.astype(F32), 0.0).astype(BF)
    n = ids.shape[1]
    spot = lax.broadcasted_iota(jnp.int32, (BAGS, n), 0)
    member = jnp.where(jnp.broadcast_to(place, (BAGS, n)) == spot, 1.0, 0.0).astype(BF)
    return dot(member, wide, 1, 0).astype(BF)


def slot_row(slots):
    owner = (slots * 6554) >> 16
    base = owner * 128 + (slots - owner * 10)
    parts = [base + 10 * t for t in range(T2N)]
    parts.append(jnp.full((1, 512 - FP * T2N), -1, jnp.int32))
    return jnp.concatenate(parts, axis=1)


def gather_fields(slots, arrived):
    col = lane_columns(slot_row(slots).astype(F32))[: FP * T2N]
    parts = []
    for b in range(BAGS // 128):
        lane = lax.broadcasted_iota(jnp.int32, col.shape, 1) + 128 * b
        parts.append(jnp.where(col == lane.astype(F32), 1.0, 0.0).astype(BF))
    chooser = jnp.concatenate(parts, axis=1)
    picked = dot(chooser, arrived, 1, 0)
    x = jnp.concatenate([picked[FP * t : FP * (t + 1)] for t in range(T2N)], axis=1)
    field = lax.broadcasted_iota(jnp.int32, x.shape, 0)
    return jnp.where(field == F, 1.0, x)


def scatter_fields(slots, grads):
    row = slot_row(slots)
    spot = lax.broadcasted_iota(jnp.int32, (BAGS, 512), 0)
    member = jnp.where(jnp.broadcast_to(row, (BAGS, 512)) == spot, 1.0, 0.0).astype(BF)
    tall = [grads[:, 128 * t : 128 * (t + 1)] for t in range(T2N)]
    tall.append(jnp.zeros((512 - FP * T2N, 128), F32))
    tall = jnp.concatenate(tall, axis=0).astype(BF)
    return dot(member, tall, 1, 0).astype(BF)


def spread_rows(ids, returned):
    place, half = bag_places(ids)
    place_col = lane_columns(place.astype(F32))
    half_col = lane_columns(half.astype(F32))
    parts = []
    for b in range(BAGS // 128):
        lane = lax.broadcasted_iota(jnp.int32, place_col.shape, 1) + 128 * b
        parts.append(jnp.where(place_col == lane.astype(F32), 1.0, 0.0).astype(BF))
    member = jnp.concatenate(parts, axis=1)
    both = dot(member, returned, 1, 0)
    return jnp.where(half_col[:, :64] == 0.0, both[:, :64], both[:, 64:]).astype(BF)


def pairs_from(full, k, stride, out, zero_tail=True):
    step = stride + 1
    low = full[pl.ds(k, F - k, stride=step), :]
    if k:
        low = low + full[pl.ds(k * stride, F - k, stride=step), :]
    out[pl.ds(FP * k, F - k), :] = low
    if k:
        high = full[pl.ds((F - k) * stride, k, stride=step), :]
        high = high + full[pl.ds(F - k, k, stride=step), :]
        out[pl.ds(FP * k + F - k, k), :] = high


def pairs_to(src, first, k, stride, full):
    step = stride + 1
    low = src[pl.ds(first + FP * k, F - k), :]
    full[pl.ds(k, F - k, stride=step), :] = low
    if k:
        full[pl.ds(k * stride, F - k, stride=step), :] = low
        high = src[pl.ds(first + FP * k + F - k, k), :]
        full[pl.ds((F - k) * stride, k, stride=step), :] = high
        full[pl.ds(F - k, k, stride=step), :] = high


def prepare(w1_ref, w2_ref, w3_ref, out_w, tall, full, sym_q, sym_w, u_ref, a_ref, at_ref):
    lane = lax.broadcasted_iota(jnp.int32, (H, 128), 1)
    sublane = lax.broadcasted_iota(jnp.int32, (H, 128), 0)
    w3_col = lane_columns(out_w[2:3, :]).astype(BF)
    tall[...] = dot(w3_ref[...], w3_col, 0, 0)
    u = jnp.where(lane == F, lane_columns(out_w[1:2, :]), 0.0)
    for i in range(F):
        u = jnp.where(lane == i, tall[pl.ds(i, H, stride=F), :], u)
    u = u.astype(BF)
    u_ref[...] = u
    eye = jnp.where(lane == sublane, 1.0, 0.0).astype(BF)
    full[pl.ds(0, F * F), :] = dot(w1_ref[...], eye, 0, 0)
    sym_w[...] = jnp.zeros_like(sym_w)
    for k in range(HALF):
        pairs_from(full, k, F, sym_w)
    tall[...] = dot(w2_ref[...], u, 0, 0)
    for i in range(F):
        block = jnp.transpose(tall[pl.ds(i, H, stride=F), :])
        full[pl.ds(FP * i, FP), :] = block[:FP]
    sym_q[...] = jnp.zeros_like(sym_q)
    for k in range(HALF):
        pairs_from(full, k, FP, sym_q)
    sym_q[pl.ds(FP * HALF, F), :] = full[pl.ds(F, F, stride=FP), :]
    sym_q[pl.ds(FP * HALF + F, 1), :] = out_w[0:1, :]
    a_ref[:, :H] = sym_q[:PAIRS].astype(BF)
    a_ref[:, H:] = sym_w[:PAIRS].astype(BF)
    for b in range(PL // 128):
        at_ref[:H, 128 * b : 128 * (b + 1)] = jnp.transpose(sym_w[128 * b : 128 * (b + 1)]).astype(BF)
        at_ref[H:, 128 * b : 128 * (b + 1)] = jnp.transpose(sym_q[128 * b : 128 * (b + 1)]).astype(BF)


def forward(x, at_ref, xx, z_ref, y_ref):
    xx[0:FP, :] = x
    xx[F : F + FP, :] = x
    ones = xx[0:FP, :]
    field = lax.broadcasted_iota(jnp.int32, (FP, LANES), 0)
    x1 = jnp.where(field == F, 1.0, ones)
    for b in range(HALF // 2):
        two = [x1 * xx[pl.ds(k, FP), :] for k in (2 * b, 2 * b + 1)]
        z_ref[pl.ds(2 * FP * b, 2 * FP), :] = jnp.concatenate(two, axis=0).astype(BF)
    z_ref[pl.ds(FP * HALF, PL - FP * HALF), :] = jnp.concatenate(
        [x1, jnp.zeros((PL - FP * HALF - FP, LANES), F32)], axis=0
    ).astype(BF)
    y_ref[...] = dot(at_ref[...], z_ref[...], 1, 0)
    total = jnp.sum(y_ref[:H, :] * y_ref[H:, :], axis=0, keepdims=True)
    total = jnp.concatenate([total[:, 128 * t : 128 * (t + 1)] for t in range(T2N)], axis=0)
    first = lax.broadcasted_iota(jnp.int32, total.shape, 1) < 64
    low = jnp.sum(jnp.where(first, total, 0.0), axis=1, keepdims=True)
    high = jnp.sum(jnp.where(first, 0.0, total), axis=1, keepdims=True)
    return jnp.where(first, low, high)


def slope_row(logits, labels_ref):
    row = lax.broadcasted_iota(jnp.int32, (T2N, 128), 0)
    lane = lax.broadcasted_iota(jnp.int32, (T2N, 128), 1)
    sample = 2 * row + (lane >= 64).astype(jnp.int32)
    labels = jnp.zeros((T2N, 128), F32)
    for n in range(2 * T2N):
        labels = jnp.where(sample == n, labels_ref[n].astype(F32), labels)
    slope = SCALE * (1.0 / (1.0 + jnp.exp(-logits)) - labels)
    return jnp.concatenate([slope[t : t + 1] for t in range(T2N)], axis=1)


def weight_sums(slope, y_ref, z_ref, sy_ref):
    sy_ref[...] = (y_ref[...] * slope).astype(BF)
    both = dot(z_ref[:PAIRS], sy_ref[...], 1, 1)
    return jnp.concatenate([both[:, :H], both[:, H:]], axis=0)


def field_grads(a_ref, sy_ref, xx, acc):
    r = dot(a_ref[...], sy_ref[...], 1, 0)
    field = lax.broadcasted_iota(jnp.int32, (FP, LANES), 0)
    acc[...] = jnp.zeros_like(acc)
    total = r[FP * HALF : FP * HALF + FP]
    x = xx[0:FP, :]
    for k in range(HALF):
        block = r[FP * k : FP * (k + 1)]
        total = total + block * xx[pl.ds(k, FP), :]
        acc[pl.ds(k, FP), :] += block * x
    total = total + acc[0:FP, :] + acc[F : F + FP, :]
    return jnp.where(field == F, 0.0, total)


def finish(sums, u_mine, w3_mine, mine, w2_ref, full, tall, g1_ref, g2_ref, g3_ref):
    lane = lax.broadcasted_iota(jnp.int32, (H, 128), 1)
    for k in range(HALF):
        pairs_to(sums, PAIRS, k, F, full)
    rows = full[pl.ds(0, F * F), :].astype(BF)
    g1_ref[...] = dot(mine, rows, 1, 1)
    for k in range(HALF):
        pairs_to(sums, 0, k, FP, full)
    full[pl.ds(F, F, stride=FP), :] = sums[pl.ds(FP * HALF, F), :]
    for i in range(F):
        block = jnp.concatenate([full[pl.ds(FP * i, FP), :], jnp.zeros((128 - FP, 128), F32)], axis=0)
        tall[pl.ds(i, H, stride=F), :] = jnp.transpose(block)
    flat = tall[...].astype(BF)
    g2_ref[...] = dot(u_mine, flat, 1, 1)
    v3 = dot(w2_ref[...], flat, 1, 0)
    for i in range(F):
        tall[pl.ds(i, H, stride=F), :] = jnp.where(lane == i, v3, 0.0)
    g3_ref[...] = dot(w3_mine, tall[...].astype(BF), 1, 1)


def params(**kw):
    return pltpu.CompilerParams(vmem_limit_bytes=60 << 20, **kw)


def k_pool(ids_ref, rows_ref, out_ref):
    out_ref[...] = pool(ids_ref[...], rows_ref[0])


def k_prep(w1_ref, w2_ref, w3_ref, ow_ref, u_ref, a_ref, at_ref, tall, full, sym_q, sym_w):
    prepare(w1_ref, w2_ref, w3_ref, ow_ref[...].astype(F32), tall, full, sym_q, sym_w, u_ref, a_ref, at_ref)


def k_forward(slots_ref, arrived_ref, at_ref, xx, z_ref, y_ref, sums_ref):
    x = gather_fields(slots_ref[...], arrived_ref[...])
    sums_ref[...] = forward(x, at_ref, xx, z_ref, y_ref)


def k_backward(labels_ref, slots_ref, logits_ref, xx, z_ref, y_ref, a_ref, sums_ref, out_ref, sy_ref, acc):
    slope = slope_row(logits_ref[...], labels_ref)
    sums_ref[...] = weight_sums(slope, y_ref, z_ref, sy_ref)
    out_ref[...] = scatter_fields(slots_ref[...], field_grads(a_ref, sy_ref, xx, acc))


def k_rows(ids_ref, returned_ref, out_ref):
    out_ref[0] = spread_rows(ids_ref[...], returned_ref[...])


def k_finish(sums_ref, u_ref, ow_ref, w2_ref, g1_ref, g2_ref, g3_ref, full, tall):
    dp = lax.axis_index("dp")
    row = lax.broadcasted_iota(jnp.int32, (8, 128), 0)
    lane = lax.broadcasted_iota(jnp.int32, (8, 128), 1)
    mine = jnp.where(lane == row + 8 * dp, 1.0, 0.0).astype(BF)
    u_mine = dot(mine, u_ref[...], 1, 0).astype(BF)
    w3 = jnp.broadcast_to(ow_ref[2:3, :].astype(F32), (8, 128))
    w3 = jnp.sum(jnp.where(lane == row + 8 * dp, w3, 0.0), axis=1, keepdims=True)
    w3_mine = jnp.broadcast_to(w3, (8, 128)).astype(BF)
    finish(sums_ref, u_mine, w3_mine, mine, w2_ref, full, tall, g1_ref, g2_ref, g3_ref)


def shape(dims, dtype):
    return jax.ShapeDtypeStruct(dims, dtype)


TALL = pltpu.VMEM((F * H, 128), F32)
FULL = pltpu.VMEM((F * FP, 128), F32)


def call(kernel, outs, specs, scratch=()):
    single = not isinstance(outs, (tuple, list))
    return pl.pallas_call(
        kernel,
        out_shape=outs,
        in_specs=specs,
        out_specs=VMEM if single else [VMEM] * len(outs),
        scratch_shapes=scratch,
        compiler_params=params(),
    )


def run_pool(ids, rows):
    return call(k_pool, shape((BAGS, 128), BF), [VMEM] * 2)(ids, rows)


def run_prep(w1, w2, w3, ow):
    sym = pltpu.VMEM((PL, 128), F32)
    outs = [shape((H, 128), BF), shape((PAIRS, 256), BF), shape((256, PL), BF)]
    return call(k_prep, outs, [VMEM] * 4, [TALL, FULL, sym, sym])(w1, w2, w3, ow)


def run_forward(slots, arrived, at):
    outs = [shape((88, LANES), F32), shape((PL, LANES), BF), shape((256, LANES), F32), shape((T2N, 128), F32)]
    return call(k_forward, outs, [VMEM] * 3)(slots, arrived, at)


def run_backward(labels, slots, logits, xx, z, y, a):
    outs = [shape((2 * PAIRS, 128), F32), shape((BAGS, 128), BF)]
    scratch = [pltpu.VMEM((256, LANES), BF), pltpu.VMEM((88, LANES), F32)]
    return call(k_backward, outs, [SMEM] + [VMEM] * 6, scratch)(labels, slots, logits, xx, z, y, a)


def run_rows(ids, returned):
    return call(k_rows, shape((1, ids.shape[1], 64), BF), [VMEM] * 2)(ids, returned)


def run_finish(sums, u, ow, w2):
    outs = [shape((8, F * F), F32), shape((8, F * H), F32), shape((8, F * H), F32)]
    return call(k_finish, outs, [VMEM] * 4, [FULL, TALL])(sums, u, ow, w2)


def local(looked_rows, bag_ids, slot_of, labels, out_weight, filter_first, filter_second, filter_third):
    slots = slot_of.reshape(1, FP)
    pooled = run_pool(bag_ids, looked_rows)
    arrived = lax.all_to_all(pooled, "samp", 0, 0, tiled=True)
    u, a, at = run_prep(filter_first, filter_second, filter_third, out_weight)
    xx, z, y, sums = run_forward(slots, arrived, at)
    logits = sums + lax.ppermute(sums, "col", [(0, 1), (1, 0)])
    weight, slot_grads = run_backward(labels, slots, logits, xx, z, y, a)
    weight = lax.psum(weight, ("dp", "samp", "col"))
    returned = lax.all_to_all(slot_grads, "samp", 0, 0, tiled=True)
    row_grads = run_rows(bag_ids, returned)
    return (row_grads, *run_finish(weight, u, out_weight, filter_second))


def solution(mesh):
    in_specs = (
        P(("dp", "samp"), None, "col"),
        P(("dp", "samp"), None),
        P(),
        P(("dp", "samp")),
        P(),
        P(),
        P(),
        P(),
    )
    out_specs = (P(("dp", "samp"), None, "col"), P("dp", None), P("dp", None), P("dp", None))
    return jax.shard_map(local, mesh=mesh, in_specs=in_specs, out_specs=out_specs, check_vma=False)
```

```python
import functools

import jax
import jax.numpy as jnp
from jax import lax
from jax.experimental import pallas as pl
from jax.experimental.pallas import tpu as pltpu
from jax.sharding import PartitionSpec as P

F = 39
FP = 40
H = 128
HALF = 20
PAIRS = 848
PL = 896
LANES = 1536
T2N = 12
BAGS = 512
SCALE = 16.0
BF = jnp.bfloat16
F32 = jnp.float32
VMEM = pl.BlockSpec(memory_space=pltpu.VMEM)
SMEM = pl.BlockSpec(memory_space=pltpu.SMEM)


def dot(a, b, ca, cb):
    return lax.dot_general(a, b, (((ca,), (cb,)), ((), ())), preferred_element_type=F32)


def lane_columns(row):
    n = row.shape[1] // 128
    blocks = [
        jnp.transpose(jnp.broadcast_to(row[:, b * 128 : (b + 1) * 128], (128, 128)))
        for b in range(n)
    ]
    return jnp.concatenate(blocks, axis=0)


def bag_places(ids):
    tens = (ids * 6554) >> 16
    twenties = (ids * 3277) >> 16
    row = twenties * 10 + (ids - tens * 10)
    row = row + 8 * ((row * 8739) >> 20)
    return row, tens - 2 * twenties


def bag_member(ids):
    place, _ = bag_places(ids)
    n = ids.shape[1]
    spot = lax.broadcasted_iota(jnp.int32, (BAGS, n), 0)
    return jnp.where(jnp.broadcast_to(place, (BAGS, n)) == spot, 1.0, 0.0).astype(BF)


def pool(ids, rows, member):
    half = bag_places(ids)[1].astype(F32)
    rows = rows.astype(F32)
    wide = jnp.concatenate([rows * (1.0 - half), rows * half], axis=0).astype(BF)
    return dot(member, wide, 1, 1).astype(BF)


def slot_row(slots):
    owner = (slots * 6554) >> 16
    base = owner * 128 + (slots - owner * 10)
    parts = [base + 10 * t for t in range(T2N)]
    parts.append(jnp.full((1, 512 - FP * T2N), -1, jnp.int32))
    return jnp.concatenate(parts, axis=1)


def gather_fields(slots, arrived):
    col = lane_columns(slot_row(slots).astype(F32))[: FP * T2N]
    parts = []
    for b in range(BAGS // 128):
        lane = lax.broadcasted_iota(jnp.int32, col.shape, 1) + 128 * b
        parts.append(jnp.where(col == lane.astype(F32), 1.0, 0.0).astype(BF))
    chooser = jnp.concatenate(parts, axis=1)
    picked = dot(chooser, arrived, 1, 0)
    x = jnp.concatenate([picked[FP * t : FP * (t + 1)] for t in range(T2N)], axis=1)
    field = lax.broadcasted_iota(jnp.int32, x.shape, 0)
    return jnp.where(field == F, 1.0, x)


def scatter_fields(slots, grads):
    row = slot_row(slots)
    spot = lax.broadcasted_iota(jnp.int32, (BAGS, 512), 0)
    member = jnp.where(jnp.broadcast_to(row, (BAGS, 512)) == spot, 1.0, 0.0).astype(BF)
    tall = [grads[:, 128 * t : 128 * (t + 1)] for t in range(T2N)]
    tall.append(jnp.zeros((512 - FP * T2N, 128), F32))
    tall = jnp.concatenate(tall, axis=0).astype(BF)
    return dot(member, tall, 1, 0).astype(BF)


def spread_rows(ids, member, returned):
    half = bag_places(ids)[1]
    both = dot(returned, member, 0, 0)
    return jnp.where(half == 0, both[:64], both[64:]).astype(BF)


def pairs_from(full, k, stride, out, zero_tail=True):
    step = stride + 1
    low = full[pl.ds(k, F - k, stride=step), :]
    if k:
        low = low + full[pl.ds(k * stride, F - k, stride=step), :]
    out[pl.ds(FP * k, F - k), :] = low
    if k:
        high = full[pl.ds((F - k) * stride, k, stride=step), :]
        high = high + full[pl.ds(F - k, k, stride=step), :]
        out[pl.ds(FP * k + F - k, k), :] = high


def pairs_to(src, first, k, stride, full):
    step = stride + 1
    low = src[pl.ds(first + FP * k, F - k), :]
    full[pl.ds(k, F - k, stride=step), :] = low
    if k:
        full[pl.ds(k * stride, F - k, stride=step), :] = low
        high = src[pl.ds(first + FP * k + F - k, k), :]
        full[pl.ds((F - k) * stride, k, stride=step), :] = high
        full[pl.ds(F - k, k, stride=step), :] = high


def prepare(w1_ref, w2_ref, w3_ref, out_w, tall, full, sym_q, sym_w, u_ref, a_ref, at_ref):
    lane = lax.broadcasted_iota(jnp.int32, (H, 128), 1)
    w3_col = lane_columns(out_w[2:3, :]).astype(BF)
    tall[...] = dot(w3_ref[...], w3_col, 0, 0)
    u = jnp.where(lane == F, lane_columns(out_w[1:2, :]), 0.0)
    for i in range(F):
        u = jnp.where(lane == i, tall[pl.ds(i, H, stride=F), :], u)
    u = u.astype(BF)
    u_ref[...] = u
    full[pl.ds(0, F * F), :] = w1_ref[...].astype(F32)
    sym_w[...] = jnp.zeros_like(sym_w)
    for k in range(HALF):
        pairs_from(full, k, F, sym_w)
    tall[...] = dot(w2_ref[...], u, 0, 0)
    for i in range(F):
        block = jnp.transpose(tall[pl.ds(i, H, stride=F), :])
        full[pl.ds(FP * i, FP), :] = block[:FP]
    sym_q[...] = jnp.zeros_like(sym_q)
    for k in range(HALF):
        pairs_from(full, k, FP, sym_q)
    sym_q[pl.ds(FP * HALF, F), :] = full[pl.ds(F, F, stride=FP), :]
    sym_q[pl.ds(FP * HALF + F, 1), :] = out_w[0:1, :]
    a_ref[:, :H] = sym_w[:PAIRS].astype(BF)
    a_ref[:, H:] = sym_q[:PAIRS].astype(BF)
    for b in range(PL // 128):
        at_ref[:H, 128 * b : 128 * (b + 1)] = jnp.transpose(sym_w[128 * b : 128 * (b + 1)]).astype(BF)
        at_ref[H:, 128 * b : 128 * (b + 1)] = jnp.transpose(sym_q[128 * b : 128 * (b + 1)]).astype(BF)


def forward(x, at_ref, xx, z_ref, y_ref):
    xx[0:FP, :] = x
    xx[F : F + FP, :] = x
    ones = xx[0:FP, :]
    field = lax.broadcasted_iota(jnp.int32, (FP, LANES), 0)
    x1 = jnp.where(field == F, 1.0, ones)
    for b in range(HALF // 2):
        two = [x1 * xx[pl.ds(k, FP), :] for k in (2 * b, 2 * b + 1)]
        z_ref[pl.ds(2 * FP * b, 2 * FP), :] = jnp.concatenate(two, axis=0).astype(BF)
    z_ref[pl.ds(FP * HALF, PL - FP * HALF), :] = jnp.concatenate(
        [x1, jnp.zeros((PL - FP * HALF - FP, LANES), F32)], axis=0
    ).astype(BF)
    y_ref[...] = dot(at_ref[...], z_ref[...], 1, 0)
    total = jnp.sum(y_ref[:H, :] * y_ref[H:, :], axis=0, keepdims=True)
    total = jnp.concatenate([total[:, 128 * t : 128 * (t + 1)] for t in range(T2N)], axis=0)
    first = lax.broadcasted_iota(jnp.int32, total.shape, 1) < 64
    low = jnp.sum(jnp.where(first, total, 0.0), axis=1, keepdims=True)
    high = jnp.sum(jnp.where(first, 0.0, total), axis=1, keepdims=True)
    return jnp.where(first, low, high)


def slope_row(logits, labels_ref):
    row = lax.broadcasted_iota(jnp.int32, (T2N, 128), 0)
    lane = lax.broadcasted_iota(jnp.int32, (T2N, 128), 1)
    sample = 2 * row + (lane >= 64).astype(jnp.int32)
    labels = jnp.zeros((T2N, 128), F32)
    for n in range(2 * T2N):
        labels = jnp.where(sample == n, labels_ref[n].astype(F32), labels)
    slope = SCALE * (1.0 / (1.0 + jnp.exp(-logits)) - labels)
    return jnp.concatenate([slope[t : t + 1] for t in range(T2N)], axis=1)


def field_grads(a_ref, y16, xx, acc):
    swapped = jnp.concatenate([y16[H:], y16[:H]], axis=0)
    r = dot(a_ref[...], swapped, 1, 0)
    field = lax.broadcasted_iota(jnp.int32, (FP, LANES), 0)
    acc[...] = jnp.zeros_like(acc)
    total = r[FP * HALF : FP * HALF + FP]
    x = xx[0:FP, :]
    for k in range(HALF):
        block = r[FP * k : FP * (k + 1)]
        total = total + block * xx[pl.ds(k, FP), :]
        acc[pl.ds(k, FP), :] += block * x
    total = total + acc[0:FP, :] + acc[F : F + FP, :]
    return jnp.where(field == F, 0.0, total)


def finish_first(g1, full, g1_ref):
    for k in range(HALF):
        pairs_to(g1, 0, k, F, full)
    row = lax.broadcasted_iota(jnp.int32, (8, 128), 0)
    lane = lax.broadcasted_iota(jnp.int32, (8, 128), 1)
    eye = jnp.where(row == lane, 1.0, 0.0).astype(BF)
    g1_ref[...] = dot(eye, full[pl.ds(0, F * F), :].astype(BF), 1, 1)


def finish_rest(t2, u_mine, w3_mine, w2_ref, full, tall, g2_ref, g3_ref):
    lane = lax.broadcasted_iota(jnp.int32, (H, 128), 1)
    for k in range(HALF):
        pairs_to(t2, 0, k, FP, full)
    full[pl.ds(F, F, stride=FP), :] = t2[pl.ds(FP * HALF, F), :]
    for i in range(F):
        block = jnp.concatenate([full[pl.ds(FP * i, FP), :], jnp.zeros((128 - FP, 128), F32)], axis=0)
        tall[pl.ds(i, H, stride=F), :] = jnp.transpose(block)
    flat = tall[...].astype(BF)
    g2_ref[...] = dot(u_mine, flat, 1, 1)
    v3 = dot(w2_ref[...], flat, 1, 0)
    for i in range(F):
        tall[pl.ds(i, H, stride=F), :] = jnp.where(lane == i, v3, 0.0)
    g3_ref[...] = dot(w3_mine, tall[...].astype(BF), 1, 1)


MESH = pl.DeviceIdType.MESH
T2ROWS = PL // 8


class Group:
    def __init__(self, n, me, device):
        self.n, self.me, self.device = n, me, device

    def others(self):
        return [lax.rem(self.me + r, self.n) for r in range(1, self.n)]

    def send(self, source, dst, sems):
        copies = []
        for r, p in enumerate(self.others()):
            copies.append(
                pltpu.make_async_remote_copy(
                    src_ref=source(p),
                    dst_ref=dst.at[self.me],
                    send_sem=sems.at[0, r],
                    recv_sem=sems.at[1, r],
                    device_id=self.device(p),
                    device_id_type=MESH,
                )
            )
            copies[-1].start()
        return copies


def arrived(copies):
    for c in copies:
        c.wait_recv()


def added(ref, n):
    total = ref[0].astype(F32)
    for p in range(1, n):
        total = total + ref[p].astype(F32)
    return total


def k_main(
    ids_ref, rows_ref, slots_ref, labels_ref, ow_ref, w1_ref, w2_ref, w3_ref,
    rg_ref, t2_ref, g1_ref, u_ref,
    w2, w3, tall, full, sym_q, sym_w, a_ref, at_ref, member, xx, z_ref, y_ref, acc,
    pooled, bags, sums, slots_out, slots_in, t2b, p1, px, py, p4, g1b, gx, gxs, gy, gz,
    load_sems, bag_sems, sum_sems, slot_sems, p1_sems, px_sems, py_sems, p4_sems, gx_sems, gy_sems, gz_sems,
):
    dp, samp, col = lax.axis_index("dp"), lax.axis_index("samp"), lax.axis_index("col")
    yy, xc = dp // 4, lax.rem(dp, 4)
    samps = Group(4, samp, lambda p: {"dp": dp, "samp": p, "col": col})
    cols = Group(2, col, lambda p: {"dp": dp, "samp": samp, "col": p})
    column = Group(8, samp * 2 + col, lambda p: {"dp": dp, "samp": p // 2, "col": lax.rem(p, 2)})
    alongx = Group(4, xc, lambda p: {"dp": yy * 4 + p, "samp": samp, "col": col})
    alongy = Group(4, yy, lambda p: {"dp": p * 4 + xc, "samp": samp, "col": col})

    loads = [
        pltpu.make_async_copy(w3_ref, w3, load_sems.at[0]),
        pltpu.make_async_copy(w2_ref, w2, load_sems.at[1]),
    ]
    for c in loads:
        c.start()
    barrier = pltpu.get_barrier_semaphore()
    for group in (column, alongx, alongy):
        for p in group.others():
            pl.semaphore_signal(barrier, inc=1, device_id=group.device(p), device_id_type=MESH)

    ids = ids_ref[...]
    member[...] = bag_member(ids)
    mine = pool(ids, rows_ref[0], member[...])
    pooled[...] = mine.reshape(4, 128, 128)
    bags[samp] = pooled[samp]
    pl.semaphore_wait(barrier, 13)
    started = samps.send(lambda p: pooled.at[p], bags, bag_sems)
    sent = started

    for c in loads:
        c.wait()
    prepare(w1_ref, w2, w3, ow_ref[...].astype(F32), tall, full, sym_q, sym_w, u_ref, a_ref, at_ref)

    arrived(started)
    x = gather_fields(slots_ref[...], bags[...].reshape(BAGS, 128))
    sums[col, :T2N] = forward(x, at_ref, xx, z_ref, y_ref)
    sums[col, T2N:] = jnp.zeros((16 - T2N, 128), F32)
    started = cols.send(lambda p: sums.at[col], sums, sum_sems)
    sent = sent + started
    grads = field_grads(a_ref, y_ref[...].astype(BF), xx, acc)
    arrived(started)
    slope = slope_row(sums[0, :T2N] + sums[1, :T2N], labels_ref)

    both = dot(z_ref[...], (y_ref[...] * slope).astype(BF), 1, 1)
    t2b[...] = both[:, :H].astype(BF).reshape(8, T2ROWS, 128)
    q = samp * 2 + col
    p1[q] = t2b[q]
    to_p1 = column.send(lambda p: t2b.at[p], p1, p1_sems)
    turned = jnp.concatenate([jnp.transpose(both[128 * b : 128 * (b + 1), H:]) for b in range(PL // 128)], axis=1)
    turned = jnp.concatenate([turned, jnp.zeros((H, 1024 - PL), F32)], axis=1)
    for d in range(16):
        block = turned[8 * d : 8 * d + 8]
        block = jnp.concatenate([block[:, :512], block[:, 512:]], axis=0).astype(BF)
        g1b[d % 4, d // 4] = block
    gx[xc] = g1b[xc]
    to_gx = alongx.send(lambda p: g1b.at[p], gx, gx_sems)
    slots_out[...] = scatter_fields(slots_ref[...], grads * slope).reshape(4, 128, 128)
    slots_in[samp] = slots_out[samp]
    to_slots = samps.send(lambda p: slots_out.at[p], slots_in, slot_sems)

    arrived(to_p1)
    px[xc] = added(p1, 8).astype(BF)
    to_px = alongx.send(lambda p: px.at[xc], px, px_sems)
    arrived(to_gx)
    gxs[...] = added(gx, 4).astype(BF)
    gy[yy] = gxs[yy]
    to_gy = alongy.send(lambda p: gxs.at[p], gy, gy_sems)
    arrived(to_px)
    py[yy] = added(px, 4).astype(BF)
    to_py = alongy.send(lambda p: py.at[yy], py, py_sems)
    arrived(to_slots)
    rg_ref[0] = spread_rows(ids, member[...], slots_in[...].reshape(BAGS, 128))
    arrived(to_gy)
    gz[q] = added(gy, 4).astype(BF)
    to_gz = column.send(lambda p: gz.at[q], gz, gz_sems)
    arrived(to_py)
    p4[q] = added(py, 4).astype(BF)
    to_p4 = column.send(lambda p: p4.at[q], p4, p4_sems)
    arrived(to_gz)
    block = added(gz, 8)
    g1_ref[...] = jnp.concatenate([block[:8], block[8:]], axis=1)
    arrived(to_p4)
    t2_ref[...] = p4[...].reshape(PL, 128).astype(F32)
    for c in sent + to_p1 + to_gx + to_slots + to_px + to_gy + to_py + to_gz + to_p4:
        c.wait_send()


def k_finish(t2_ref, g1_in, u_ref, ow_ref, w2_ref, g1_ref, g2_ref, g3_ref, full, tall, first):
    dp = lax.axis_index("dp")
    row = lax.broadcasted_iota(jnp.int32, (8, 128), 0)
    lane = lax.broadcasted_iota(jnp.int32, (8, 128), 1)
    mine = jnp.where(lane == row + 8 * dp, 1.0, 0.0).astype(BF)
    u_mine = dot(mine, u_ref[...], 1, 0).astype(BF)
    w3 = jnp.broadcast_to(ow_ref[2:3, :].astype(F32), (8, 128))
    w3 = jnp.sum(jnp.where(lane == row + 8 * dp, w3, 0.0), axis=1, keepdims=True)
    w3_mine = jnp.broadcast_to(w3, (8, 128)).astype(BF)
    tail = jnp.zeros((120, 128), F32)
    for b in range(PL // 128):
        block = jnp.concatenate([g1_in[:, 128 * b : 128 * (b + 1)], tail], axis=0)
        first[pl.ds(128 * b, 128), :] = jnp.transpose(block)
    finish_first(first, full, g1_ref)
    finish_rest(t2_ref, u_mine, w3_mine, w2_ref, full, tall, g2_ref, g3_ref)


def shape(dims, dtype):
    return jax.ShapeDtypeStruct(dims, dtype)


TALL = pltpu.VMEM((F * H, 128), F32)
FULL = pltpu.VMEM((F * FP, 128), F32)
ANY = pl.BlockSpec(memory_space=pl.ANY)


def pair_sems(n):
    return pltpu.SemaphoreType.DMA((2, n - 1))


def run_main(ids, rows, slots, labels, ow, w1, w2, w3):
    n = ids.shape[1]
    vm = pltpu.VMEM
    sym = vm((PL, 128), F32)
    scratch = [
        vm((H, F * H), BF), vm((H, F * H), BF), TALL, FULL, sym, sym,
        vm((PAIRS, 256), BF), vm((256, PL), BF), vm((BAGS, n), BF),
        vm((88, LANES), F32), vm((PL, LANES), BF), vm((256, LANES), F32), vm((88, LANES), F32),
        vm((4, 128, 128), BF), vm((4, 128, 128), BF), vm((2, 16, 128), F32),
        vm((4, 128, 128), BF), vm((4, 128, 128), BF),
        vm((8, T2ROWS, 128), BF), vm((8, T2ROWS, 128), BF), vm((4, T2ROWS, 128), BF), vm((4, T2ROWS, 128), BF), vm((8, T2ROWS, 128), BF),
        vm((4, 4, 16, 512), BF), vm((4, 4, 16, 512), BF), vm((4, 16, 512), BF), vm((4, 16, 512), BF), vm((8, 16, 512), BF),
        pltpu.SemaphoreType.DMA((2,)),
        pair_sems(4), pair_sems(2), pair_sems(4), pair_sems(8), pair_sems(4), pair_sems(4), pair_sems(8),
        pair_sems(4), pair_sems(4), pair_sems(8),
    ]
    return pl.pallas_call(
        k_main,
        out_shape=[shape((1, 64, n), BF), shape((PL, 128), F32), shape((8, 1024), F32), shape((H, 128), BF)],
        in_specs=[VMEM, VMEM, VMEM, SMEM, VMEM, VMEM, ANY, ANY],
        out_specs=[VMEM] * 4,
        scratch_shapes=scratch,
        compiler_params=pltpu.CompilerParams(collective_id=0, has_side_effects=True, vmem_limit_bytes=60 << 20),
    )(ids, rows, slots, labels, ow, w1, w2, w3)


def run_finish(t2, g1, u, ow, w2):
    return pl.pallas_call(
        k_finish,
        out_shape=[shape((8, F * F), F32), shape((8, F * H), F32), shape((8, F * H), F32)],
        in_specs=[VMEM] * 5,
        out_specs=[VMEM] * 3,
        scratch_shapes=[FULL, TALL, pltpu.VMEM((PL, 128), F32)],
        compiler_params=pltpu.CompilerParams(vmem_limit_bytes=60 << 20),
    )(t2, g1, u, ow, w2)


def local(looked_rows, bag_ids, slot_of, labels, out_weight, filter_first, filter_second, filter_third):
    rows, t2, g1, u = run_main(
        bag_ids, jnp.swapaxes(looked_rows, 1, 2), slot_of.reshape(1, FP), labels, out_weight,
        filter_first.T, filter_second, filter_third,
    )
    return (jnp.swapaxes(rows, 1, 2), *run_finish(t2, g1, u, out_weight, filter_second))


def solution(mesh):
    in_specs = (
        P(("dp", "samp"), None, "col"),
        P(("dp", "samp"), None),
        P(),
        P(("dp", "samp")),
        P(),
        P(),
        P(),
        P(),
    )
    out_specs = (P(("dp", "samp"), None, "col"), P("dp", None), P("dp", None), P("dp", None))
    return jax.shard_map(local, mesh=mesh, in_specs=in_specs, out_specs=out_specs, check_vma=False)
```

```python
import functools

import jax
import jax.numpy as jnp
from jax import lax
from jax.experimental import pallas as pl
from jax.experimental.pallas import tpu as pltpu
from jax.sharding import PartitionSpec as P

F = 39
FP = 40
H = 128
HALF = 20
PAIRS = 848
PL = 896
LANES = 1536
T2N = 12
BAGS = 512
CHUNK = 64
T2D = 6
SCALE = 16.0
BF = jnp.bfloat16
F32 = jnp.float32
VMEM = pl.BlockSpec(memory_space=pltpu.VMEM)
SMEM = pl.BlockSpec(memory_space=pltpu.SMEM)


def dot(a, b, ca, cb):
    return lax.dot_general(a, b, (((ca,), (cb,)), ((), ())), preferred_element_type=F32)


def lane_columns(row):
    n = row.shape[1] // 128
    blocks = [
        jnp.transpose(jnp.broadcast_to(row[:, b * 128 : (b + 1) * 128], (128, 128)))
        for b in range(n)
    ]
    return jnp.concatenate(blocks, axis=0)


def bag_places(ids):
    tens = (ids * 6554) >> 16
    twenties = (ids * 3277) >> 16
    row = twenties * 10 + (ids - tens * 10)
    row = row + 4 * ((row * 17477) >> 20)
    return row, tens - 2 * twenties


def bag_member(ids):
    place, _ = bag_places(ids)
    n = ids.shape[1]
    spot = lax.broadcasted_iota(jnp.int32, (BAGS, n), 0)
    return jnp.where(jnp.broadcast_to(place, (BAGS, n)) == spot, 1.0, 0.0).astype(BF)


def pool(ids, rows, member):
    half = bag_places(ids)[1].astype(F32)
    rows = rows.astype(F32)
    wide = jnp.concatenate([rows * (1.0 - half), rows * half], axis=0).astype(BF)
    return dot(member, wide, 1, 1).astype(BF)


def slot_row(slots):
    owner = (slots * 6554) >> 16
    base = owner * CHUNK + (slots - owner * 10)
    parts = [base + 10 * t for t in range(T2D)]
    parts.append(jnp.full((1, 256 - FP * T2D), -1, jnp.int32))
    return jnp.concatenate(parts, axis=1)


def gather_fields(slots, bags):
    col = lane_columns(slot_row(slots).astype(F32))[: FP * T2D]
    parts = []
    for b in range(2):
        lane = lax.broadcasted_iota(jnp.int32, col.shape, 1) + 128 * b
        parts.append(jnp.where(col == lane.astype(F32), 1.0, 0.0).astype(BF))
    chooser = jnp.concatenate(parts, axis=1)
    wide = jnp.concatenate([bags[:, h].reshape(4 * CHUNK, 128) for h in range(2)], axis=1)
    picked = dot(chooser, wide, 1, 0)
    x = jnp.concatenate([picked[FP * t : FP * (t + 1)] for t in range(T2D)], axis=1)
    field = lax.broadcasted_iota(jnp.int32, x.shape, 0)
    return jnp.where(field == F, 1.0, x)


def scatter_fields(slots, grads):
    row = slot_row(slots)
    spot = lax.broadcasted_iota(jnp.int32, (4 * CHUNK, 256), 0)
    member = jnp.where(jnp.broadcast_to(row, (4 * CHUNK, 256)) == spot, 1.0, 0.0).astype(BF)
    tall = [grads[:, 256 * t : 256 * (t + 1)] for t in range(T2D)]
    tall.append(jnp.zeros((256 - FP * T2D, 256), F32))
    both = dot(member, jnp.concatenate(tall, axis=0).astype(BF), 1, 0).astype(BF)
    return both[:, :128], both[:, 128:]


def spread_rows(ids, member, returned):
    half = bag_places(ids)[1]
    both = dot(returned, member, 0, 0)
    return jnp.where(half == 0, both[:64], both[64:]).astype(BF)


def pairs_from(full, k, stride, out, zero_tail=True):
    step = stride + 1
    low = full[pl.ds(k, F - k, stride=step), :]
    if k:
        low = low + full[pl.ds(k * stride, F - k, stride=step), :]
    out[pl.ds(FP * k, F - k), :] = low
    if k:
        high = full[pl.ds((F - k) * stride, k, stride=step), :]
        high = high + full[pl.ds(F - k, k, stride=step), :]
        out[pl.ds(FP * k + F - k, k), :] = high


def pairs_to(src, first, k, stride, full):
    step = stride + 1
    low = src[pl.ds(first + FP * k, F - k), :]
    full[pl.ds(k, F - k, stride=step), :] = low
    if k:
        full[pl.ds(k * stride, F - k, stride=step), :] = low
        high = src[pl.ds(first + FP * k + F - k, k), :]
        full[pl.ds((F - k) * stride, k, stride=step), :] = high
        full[pl.ds(F - k, k, stride=step), :] = high


def prepare_first(w1_ref, w3_ref, out_w, tall, full, sym_w, u_ref):
    lane = lax.broadcasted_iota(jnp.int32, (H, 128), 1)
    w3_col = lane_columns(out_w[2:3, :]).astype(BF)
    tall[...] = dot(w3_ref[...], w3_col, 0, 0)
    u = jnp.where(lane == F, lane_columns(out_w[1:2, :]), 0.0)
    for i in range(F):
        u = jnp.where(lane == i, tall[pl.ds(i, H, stride=F), :], u)
    u = u.astype(BF)
    u_ref[...] = u
    full[pl.ds(0, F * F), :] = w1_ref[...].astype(F32)
    sym_w[...] = jnp.zeros_like(sym_w)
    for k in range(HALF):
        pairs_from(full, k, F, sym_w)


def prepare_rest(w2_ref, out_w, tall, full, sym_q, sym_w, u_ref, w2p_ref, a_ref, at_ref):
    lane = lax.broadcasted_iota(jnp.int32, (H, 128), 1)
    sublane = lax.broadcasted_iota(jnp.int32, (H, 128), 0)
    tall[...] = dot(w2_ref[...], jnp.where(lane == sublane, 1.0, 0.0).astype(BF), 0, 0)
    for i in range(F):
        w2p_ref[pl.ds(H * i, H), :] = tall[pl.ds(i, H, stride=F), :].astype(BF)
    turned = jnp.transpose(u_ref[...].astype(F32))[:FP].astype(BF)
    blocks = dot(turned, w2p_ref[...], 1, 1)
    for i in range(F):
        full[pl.ds(FP * i, FP), :] = blocks[:, H * i : H * (i + 1)]
    sym_q[...] = jnp.zeros_like(sym_q)
    for k in range(HALF):
        pairs_from(full, k, FP, sym_q)
    sym_q[pl.ds(FP * HALF, F), :] = full[pl.ds(F, F, stride=FP), :]
    sym_q[pl.ds(FP * HALF + F, 1), :] = out_w[0:1, :]
    a_ref[:, :H] = sym_w[:PAIRS].astype(BF)
    a_ref[:, H:] = sym_q[:PAIRS].astype(BF)
    for b in range(PL // 128):
        at_ref[:H, 128 * b : 128 * (b + 1)] = jnp.transpose(sym_w[128 * b : 128 * (b + 1)]).astype(BF)
        at_ref[H:, 128 * b : 128 * (b + 1)] = jnp.transpose(sym_q[128 * b : 128 * (b + 1)]).astype(BF)


def forward(x, at_ref, xx, z_ref, y_ref):
    xx[0:FP, :] = x
    xx[F : F + FP, :] = x
    ones = xx[0:FP, :]
    field = lax.broadcasted_iota(jnp.int32, (FP, LANES), 0)
    x1 = jnp.where(field == F, 1.0, ones)
    for b in range(HALF // 2):
        two = [x1 * xx[pl.ds(k, FP), :] for k in (2 * b, 2 * b + 1)]
        z_ref[pl.ds(2 * FP * b, 2 * FP), :] = jnp.concatenate(two, axis=0).astype(BF)
    z_ref[pl.ds(FP * HALF, PL - FP * HALF), :] = jnp.concatenate(
        [x1, jnp.zeros((PL - FP * HALF - FP, LANES), F32)], axis=0
    ).astype(BF)
    y_ref[...] = dot(at_ref[...], z_ref[...], 1, 0)
    total = jnp.sum(y_ref[:H, :] * y_ref[H:, :], axis=0, keepdims=True)
    total = jnp.concatenate([total[:, 128 * t : 128 * (t + 1)] for t in range(T2N)], axis=0)
    total = jnp.concatenate(
        [total[2 * t : 2 * t + 1] + total[2 * t + 1 : 2 * t + 2] for t in range(T2D)], axis=0
    )
    first = lax.broadcasted_iota(jnp.int32, total.shape, 1) < 64
    low = jnp.sum(jnp.where(first, total, 0.0), axis=1, keepdims=True)
    high = jnp.sum(jnp.where(first, 0.0, total), axis=1, keepdims=True)
    return jnp.where(first, low, high)


def slope_row(logits, labels_ref, first):
    row = lax.broadcasted_iota(jnp.int32, logits.shape, 0)
    lane = lax.broadcasted_iota(jnp.int32, logits.shape, 1)
    sample = 2 * row + (lane >= 64).astype(jnp.int32)
    labels = jnp.zeros(logits.shape, F32)
    for n in range(2 * T2D):
        labels = jnp.where(sample == n, labels_ref[first + n].astype(F32), labels)
    slope = SCALE * (1.0 / (1.0 + jnp.exp(-logits)) - labels)
    return jnp.concatenate([slope[t // 2 : t // 2 + 1] for t in range(T2N)], axis=1)


def field_grads(a_ref, y16, xx, acc):
    swapped = jnp.concatenate([y16[H:], y16[:H]], axis=0)
    r = dot(a_ref[...], swapped, 1, 0)
    field = lax.broadcasted_iota(jnp.int32, (FP, LANES), 0)
    acc[...] = jnp.zeros_like(acc)
    total = r[FP * HALF : FP * HALF + FP]
    x = xx[0:FP, :]
    for k in range(HALF):
        block = r[FP * k : FP * (k + 1)]
        total = total + block * xx[pl.ds(k, FP), :]
        acc[pl.ds(k, FP), :] += block * x
    total = total + acc[0:FP, :] + acc[F : F + FP, :]
    return jnp.where(field == F, 0.0, total)


def finish_first(sums, mine, full, g1_ref):
    for k in range(HALF):
        pairs_to(sums, PAIRS, k, F, full)
    g1_ref[...] = dot(mine, full[pl.ds(0, F * F), :].astype(BF), 1, 1)


def finish_rest(t2, u_mine, w3_mine, w2p_ref, full, tall, g2_ref, g3_ref):
    for k in range(HALF):
        pairs_to(t2, 0, k, FP, full)
    full[pl.ds(F, F, stride=FP), :] = t2[pl.ds(FP * HALF, F), :]
    wide = jnp.concatenate([full[pl.ds(FP * i, FP), :] for i in range(F)], axis=1).astype(BF)
    two = dot(u_mine[:, :FP], wide, 1, 0)
    v3 = dot(wide, w2p_ref[...], 1, 0)
    rows = []
    for i in range(F):
        rows.append(two[:, H * i : H * (i + 1)])
        rows.append(w3_mine * v3[i : i + 1])
    rows.append(jnp.zeros((16, 128), F32))
    lane = lax.broadcasted_iota(jnp.int32, (H, 128), 1) // 16
    for b in range(5):
        block = jnp.transpose(jnp.concatenate(rows[16 * b : 16 * (b + 1)], axis=0))
        for i in range(8 * b, min(8 * b + 8, F)):
            tall[pl.ds(i, H, stride=F), :] = jnp.where(lane == i - 8 * b, block, 0.0)
    row = lax.broadcasted_iota(jnp.int32, (16, 128), 0)
    pick = jnp.where(lax.broadcasted_iota(jnp.int32, (16, 128), 1) % 16 == row, 1.0, 0.0).astype(BF)
    out = dot(pick, tall[...].astype(BF), 1, 1)
    g2_ref[...] = out[:8]
    g3_ref[...] = out[8:]


MESH = pl.DeviceIdType.MESH
SUMROWS = 1664
CUTS = (0, 512, 1024, SUMROWS)


class Group:
    def __init__(self, n, me, device):
        self.n, self.me, self.device = n, me, device

    def others(self):
        return [lax.rem(self.me + r, self.n) for r in range(1, self.n)]

    def send(self, source, dst, sems):
        copies = []
        for r, p in enumerate(self.others()):
            copies.append(
                pltpu.make_async_remote_copy(
                    src_ref=source(p),
                    dst_ref=dst.at[self.me],
                    send_sem=sems.at[0, r],
                    recv_sem=sems.at[1, r],
                    device_id=self.device(p),
                    device_id_type=MESH,
                )
            )
            copies[-1].start()
        return copies


def arrived(copies):
    for c in copies:
        c.wait_recv()


def added(ref, n):
    total = ref[0].astype(F32)
    for p in range(1, n):
        total = total + ref[p].astype(F32)
    return total


def k_main(
    ids_in, rows_in, slots_in_ref, labels_in, ow_in, w1_in, w2_in, w3_in,
    rg_out, w2p_out, sums_ref, um_ref, mine_ref, w3m_ref,
    ids_ref, rows_ref, slots_ref, labels_ref, ow_ref, w1_ref, w2, w3, tall, full, sym_q, sym_w, u_ref,
    w2p, rg, a_ref, at_ref, member, xx, z_ref, y_ref, acc,
    pooled, bags, slots_out, slots_in, *rest,
):
    parts = [rest[5 * i : 5 * i + 5] for i in range(3)]
    sems = [rest[15 + 4 * i : 19 + 4 * i] for i in range(3)]
    load_sems, store_sems, bag_sems, slot_sems = rest[27:]
    dp, samp, col = lax.axis_index("dp"), lax.axis_index("samp"), lax.axis_index("col")
    yy, xc = dp // 4, lax.rem(dp, 4)
    zz, core = col * 2 + samp // 2, lax.rem(samp, 2)
    q = samp * 2 + col

    def device(x=xc, y=yy, z=zz, c=core):
        return {"dp": y * 4 + x, "samp": lax.rem(z, 2) * 2 + c, "col": z // 2}

    column = Group(8, q, lambda p: {"dp": dp, "samp": p // 2, "col": lax.rem(p, 2)})
    x4 = Group(4, xc, lambda p: device(x=p))
    y4 = Group(4, yy, lambda p: device(y=p))
    z4 = Group(4, zz, lambda p: device(z=p))
    x8 = Group(8, xc * 2 + core, lambda p: device(x=p // 2, c=lax.rem(p, 2)))
    y8 = Group(8, yy * 2 + core, lambda p: device(y=p // 2, c=lax.rem(p, 2)))
    z8 = Group(8, zz * 2 + core, lambda p: device(z=p // 2, c=lax.rem(p, 2)))
    orders = ((z8, x4, y4), (x8, y4, z4), (y8, z4, x4))

    barrier = pltpu.get_barrier_semaphore()
    for p in column.others():
        pl.semaphore_signal(barrier, inc=1, device_id=column.device(p), device_id_type=MESH)
    for r in range(1, 4):
        for c in range(2):
            for peer in (device(x=lax.rem(xc + r, 4), c=c), device(y=lax.rem(yy + r, 4), c=c)):
                pl.semaphore_signal(barrier, inc=1, device_id=peer, device_id_type=MESH)
    loads = []
    for n, (source, target) in enumerate((
        (ids_in, ids_ref), (rows_in, rows_ref), (ow_in, ow_ref), (w3_in, w3), (w1_in, w1_ref), (w2_in, w2),
        (slots_in_ref, slots_ref), (labels_in, labels_ref),
    )):
        loads.append(pltpu.make_async_copy(source, target, load_sems.at[n]))
        loads[-1].start()
    loads[0].wait()
    loads[1].wait()

    ids = ids_ref[...]
    member[...] = bag_member(ids)
    pooled[...] = pool(ids, rows_ref[0], member[...]).reshape(8, CHUNK, 128)
    bags[q] = pooled[q]
    for c in loads[2:]:
        c.wait()
    out_w = ow_ref[...].astype(F32)
    prepare_first(w1_ref, w3, out_w, tall, full, sym_w, u_ref)
    pl.semaphore_wait(barrier, 19)
    to_bags = column.send(lambda p: pooled.at[p], bags, bag_sems)
    prepare_rest(w2, out_w, tall, full, sym_q, sym_w, u_ref, w2p, a_ref, at_ref)
    stores = [pltpu.make_async_copy(w2p, w2p_out, store_sems.at[0])]
    stores[0].start()
    row = lax.broadcasted_iota(jnp.int32, (8, 128), 0)
    lane = lax.broadcasted_iota(jnp.int32, (8, 128), 1)
    mine = jnp.where(lane == row + 8 * dp, 1.0, 0.0)
    mine_ref[...] = mine
    um_ref[...] = dot(mine.astype(BF), u_ref[...], 1, 0)
    w3_mine = jnp.sum(mine * out_w[2:3, :], axis=1, keepdims=True)
    w3m_ref[...] = jnp.broadcast_to(w3_mine, (8, 128))

    arrived(to_bags)
    x = gather_fields(slots_ref[...], bags[...].reshape(4, 2, CHUNK, 128))
    slope = slope_row(forward(x, at_ref, xx, z_ref, y_ref), labels_ref, 12 * col)
    both = dot(z_ref[...], (y_ref[...] * slope).astype(BF), 1, 1)
    flat = jnp.concatenate(
        [both[:PAIRS, :H], both[: FP * HALF, H:], jnp.zeros((SUMROWS - PAIRS - FP * HALF, 128), F32)], axis=0
    ).astype(BF)
    sent = list(to_bags)
    flying = []
    for i, (part, order) in enumerate(zip(parts, orders)):
        whole, landed = part[0], part[1]
        whole[...] = flat[CUTS[i] : CUTS[i + 1]].reshape(whole.shape)
        landed[order[0].me] = whole[order[0].me]
        flying.append(order[0].send(lambda p, whole=whole: whole.at[p], landed, sems[i][0]))
    grads = field_grads(a_ref, y_ref[...].astype(BF), xx, acc) * slope
    halves = scatter_fields(slots_ref[...], grads)
    for owner in range(4):
        for h in range(2):
            slots_out[2 * owner + h] = halves[h][CHUNK * owner : CHUNK * (owner + 1)]
    slots_in[q] = slots_out[q]
    to_slots = column.send(lambda p: slots_out.at[p], slots_in, slot_sems)
    sent = sent + to_slots

    for stage in range(1, 4):
        if stage == 3:
            arrived(to_slots)
        for i, (part, order) in enumerate(zip(parts, orders)):
            arrived(flying[i])
            sent = sent + flying[i]
            group = order[stage] if stage < 3 else order[0]
            source, landed = part[stage], part[stage + 1]
            landed[group.me] = added(source, 8 if stage == 1 else 4).astype(BF)
            flying[i] = group.send(lambda p, landed=landed, me=group.me: landed.at[me], landed, sems[i][stage])
    rg[0] = spread_rows(ids, member[...], slots_in[...].reshape(BAGS, 128))
    stores.append(pltpu.make_async_copy(rg, rg_out, store_sems.at[1]))
    stores[1].start()
    for i, part in enumerate(parts):
        arrived(flying[i])
        sent = sent + flying[i]
        sums_ref[pl.ds(CUTS[i], CUTS[i + 1] - CUTS[i]), :] = part[4][...].reshape(CUTS[i + 1] - CUTS[i], 128)
    for c in stores:
        c.wait()
    for c in sent:
        c.wait_send()


def shape(dims, dtype):
    return jax.ShapeDtypeStruct(dims, dtype)


TALL = pltpu.VMEM((F * H, 128), F32)
FULL = pltpu.VMEM((F * FP, 128), F32)
ANY = pl.BlockSpec(memory_space=pl.ANY)


def pair_sems(n):
    return pltpu.SemaphoreType.DMA((2, n - 1))


def run_main(ids, rows, slots, labels, ow, w1, w2, w3):
    n = ids.shape[1]
    vm = pltpu.VMEM
    sym = vm((PL, 128), F32)
    scratch = [
        vm(ids.shape, jnp.int32), vm(rows.shape, BF), vm(slots.shape, jnp.int32), pltpu.SMEM(labels.shape, jnp.int32),
        vm(ow.shape, BF), vm(w1.shape, BF), vm((H, F * H), BF), vm((H, F * H), BF), TALL, FULL, sym, sym, vm((H, 128), BF),
        vm((F * H, 128), BF), vm((1, 64, n), BF), vm((PAIRS, 256), BF), vm((256, PL), BF), vm((BAGS, n), BF),
        vm((88, LANES), F32), vm((PL, LANES), BF), vm((256, LANES), F32), vm((88, LANES), F32),
        vm((8, CHUNK, 128), BF), vm((8, CHUNK, 128), BF), vm((8, CHUNK, 128), BF), vm((8, CHUNK, 128), BF),
    ]
    for low, high in zip(CUTS, CUTS[1:]):
        scratch += [vm((k, (high - low) // 8, 128), BF) for k in (8, 8, 4, 4, 8)]
    scratch += [pair_sems(k) for _ in range(3) for k in (8, 4, 4, 8)]
    scratch += [pltpu.SemaphoreType.DMA((8,)), pltpu.SemaphoreType.DMA((2,)), pair_sems(8), pair_sems(8)]
    return pl.pallas_call(
        k_main,
        out_shape=[
            shape((1, 64, n), BF), shape((F * H, 128), BF), shape((SUMROWS, 128), BF),
            shape((8, 128), F32), shape((8, 128), F32), shape((8, 128), F32),
        ],
        in_specs=[ANY] * 8,
        out_specs=[ANY, ANY] + [VMEM] * 4,
        scratch_shapes=scratch,
        compiler_params=pltpu.CompilerParams(collective_id=0, has_side_effects=True, vmem_limit_bytes=58 << 20),
    )(ids, rows, slots, labels, ow, w1, w2, w3)


def k_finish(
    rows_in, w2p_in, sums_in, um_ref, mine_ref, w3m_ref,
    rg_out, g1_ref, g2_ref, g3_ref,
    full, tall, sums, w2p, rows, sems,
):
    copies = [
        pltpu.make_async_copy(w2p_in, w2p, sems.at[0]),
        pltpu.make_async_copy(rows_in, rows, sems.at[1]),
        pltpu.make_async_copy(rows, rg_out, sems.at[2]),
    ]
    for c in copies[:2]:
        c.start()
    sums[...] = sums_in[...].astype(F32)
    finish_first(sums, mine_ref[...].astype(BF), full, g1_ref)
    copies[1].wait()
    copies[2].start()
    copies[0].wait()
    finish_rest(sums, um_ref[...].astype(BF), w3m_ref[...], w2p, full, tall, g2_ref, g3_ref)
    copies[2].wait()


def run_finish(rows, w2p, sums, um, mine, w3m):
    return pl.pallas_call(
        k_finish,
        out_shape=[
            shape(rows.shape, BF), shape((8, F * F), F32), shape((8, F * H), F32), shape((8, F * H), F32)
        ],
        in_specs=[ANY, ANY] + [VMEM] * 4,
        out_specs=[ANY] + [VMEM] * 3,
        scratch_shapes=[
            FULL, TALL, pltpu.VMEM(sums.shape, F32), pltpu.VMEM(w2p.shape, BF),
            pltpu.VMEM(rows.shape, BF), pltpu.SemaphoreType.DMA((3,)),
        ],
        compiler_params=pltpu.CompilerParams(vmem_limit_bytes=60 << 20),
    )(rows, w2p, sums, um, mine, w3m)


def local(looked_rows, bag_ids, slot_of, labels, out_weight, filter_first, filter_second, filter_third):
    parts = run_main(
        bag_ids, jnp.swapaxes(looked_rows, 1, 2), slot_of.reshape(1, FP), labels, out_weight,
        filter_first.T, filter_second, filter_third,
    )
    rows, first, second, third = run_finish(*parts)
    return jnp.swapaxes(rows, 1, 2), first, second, third


def solution(mesh):
    in_specs = (
        P(("dp", "samp"), None, "col"),
        P(("dp", "samp"), None),
        P(),
        P(("dp", "samp")),
        P(),
        P(),
        P(),
        P(),
    )
    out_specs = (P(("dp", "samp"), None, "col"), P("dp", None), P("dp", None), P("dp", None))
    return jax.shard_map(local, mesh=mesh, in_specs=in_specs, out_specs=out_specs, check_vma=False)
```

```python
import functools

import jax
import jax.numpy as jnp
from jax import lax
from jax.experimental import pallas as pl
from jax.experimental.pallas import tpu as pltpu
from jax.sharding import PartitionSpec as P

F = 39
FP = 40
H = 128
HALF = 20
PAIRS = 848
PL = 896
LANES = 1536
T2N = 12
BAGS = 512
CHUNK = 64
T2D = 6
SCALE = 16.0
BF = jnp.bfloat16
F32 = jnp.float32
VMEM = pl.BlockSpec(memory_space=pltpu.VMEM)
SMEM = pl.BlockSpec(memory_space=pltpu.SMEM)


def dot(a, b, ca, cb):
    return lax.dot_general(a, b, (((ca,), (cb,)), ((), ())), preferred_element_type=F32)


def lane_columns(row):
    n = row.shape[1] // 128
    blocks = [
        jnp.transpose(jnp.broadcast_to(row[:, b * 128 : (b + 1) * 128], (128, 128)))
        for b in range(n)
    ]
    return jnp.concatenate(blocks, axis=0)


def bag_places(ids):
    tens = (ids * 6554) >> 16
    twenties = (ids * 3277) >> 16
    row = twenties * 10 + (ids - tens * 10)
    row = row + 4 * ((row * 17477) >> 20)
    return row, tens - 2 * twenties


def bag_member(ids):
    place, _ = bag_places(ids)
    n = ids.shape[1]
    spot = lax.broadcasted_iota(jnp.int32, (BAGS, n), 0)
    return jnp.where(jnp.broadcast_to(place, (BAGS, n)) == spot, 1.0, 0.0).astype(BF)


def pool(ids, rows, member):
    half = bag_places(ids)[1].astype(F32)
    rows = rows.astype(F32)
    wide = jnp.concatenate([rows * (1.0 - half), rows * half], axis=0).astype(BF)
    return dot(member, wide, 1, 1).astype(BF)


def slot_row(slots):
    owner = (slots * 6554) >> 16
    base = owner * CHUNK + (slots - owner * 10)
    parts = [base + 10 * t for t in range(T2D)]
    parts.append(jnp.full((1, 256 - FP * T2D), -1, jnp.int32))
    return jnp.concatenate(parts, axis=1)


def field_chooser(slots):
    col = lane_columns(slot_row(slots).astype(F32))[: FP * T2D]
    parts = []
    for b in range(2):
        lane = lax.broadcasted_iota(jnp.int32, col.shape, 1) + 128 * b
        parts.append(jnp.where(col == lane.astype(F32), 1.0, 0.0).astype(BF))
    return jnp.concatenate(parts, axis=1)


def gather_fields(chooser, bags):
    wide = jnp.concatenate([bags[:, h].reshape(4 * CHUNK, 128) for h in range(2)], axis=1)
    picked = dot(chooser, wide, 1, 0)
    x = jnp.concatenate([picked[FP * t : FP * (t + 1)] for t in range(T2D)], axis=1)
    field = lax.broadcasted_iota(jnp.int32, x.shape, 0)
    return jnp.where(field == F, 1.0, x)


def scatter_fields(slots, grads):
    row = slot_row(slots)
    spot = lax.broadcasted_iota(jnp.int32, (4 * CHUNK, 256), 0)
    member = jnp.where(jnp.broadcast_to(row, (4 * CHUNK, 256)) == spot, 1.0, 0.0).astype(BF)
    tall = [grads[:, 256 * t : 256 * (t + 1)] for t in range(T2D)]
    tall.append(jnp.zeros((256 - FP * T2D, 256), F32))
    both = dot(member, jnp.concatenate(tall, axis=0).astype(BF), 1, 0).astype(BF)
    return both[:, :128], both[:, 128:]


def spread_rows(ids, member, returned):
    half = bag_places(ids)[1]
    both = dot(returned, member, 0, 0)
    return jnp.where(half == 0, both[:64], both[64:]).astype(BF)


def pairs_from(full, k, stride, out, zero_tail=True):
    step = stride + 1
    low = full[pl.ds(k, F - k, stride=step), :]
    if k:
        low = low + full[pl.ds(k * stride, F - k, stride=step), :]
    out[pl.ds(FP * k, F - k), :] = low
    if k:
        high = full[pl.ds((F - k) * stride, k, stride=step), :]
        high = high + full[pl.ds(F - k, k, stride=step), :]
        out[pl.ds(FP * k + F - k, k), :] = high


def pairs_to(src, first, k, stride, full):
    step = stride + 1
    low = src[pl.ds(first + FP * k, F - k), :]
    full[pl.ds(k, F - k, stride=step), :] = low
    if k:
        full[pl.ds(k * stride, F - k, stride=step), :] = low
        high = src[pl.ds(first + FP * k + F - k, k), :]
        full[pl.ds((F - k) * stride, k, stride=step), :] = high
        full[pl.ds(F - k, k, stride=step), :] = high


def prepare_first(w1_ref, w3_ref, out_w, tall, full, sym_w, u_ref):
    lane = lax.broadcasted_iota(jnp.int32, (H, 128), 1)
    w3_col = lane_columns(out_w[2:3, :]).astype(BF)
    tall[...] = dot(w3_ref[...], w3_col, 0, 0)
    u = jnp.where(lane == F, lane_columns(out_w[1:2, :]), 0.0)
    for i in range(F):
        u = jnp.where(lane == i, tall[pl.ds(i, H, stride=F), :], u)
    u = u.astype(BF)
    u_ref[...] = u
    full[pl.ds(0, F * F), :] = w1_ref[...].astype(F32)
    sym_w[...] = jnp.zeros_like(sym_w)
    for k in range(HALF):
        pairs_from(full, k, F, sym_w)


def prepare_rest(w2_ref, out_w, tall, full, sym_q, sym_w, u_ref, w2p_ref, a_ref, at_ref):
    lane = lax.broadcasted_iota(jnp.int32, (H, 128), 1)
    sublane = lax.broadcasted_iota(jnp.int32, (H, 128), 0)
    tall[...] = dot(w2_ref[...], jnp.where(lane == sublane, 1.0, 0.0).astype(BF), 0, 0)
    for i in range(F):
        w2p_ref[pl.ds(H * i, H), :] = tall[pl.ds(i, H, stride=F), :].astype(BF)
    turned = jnp.transpose(u_ref[...].astype(F32))[:FP].astype(BF)
    blocks = dot(turned, w2p_ref[...], 1, 1)
    for i in range(F):
        full[pl.ds(FP * i, FP), :] = blocks[:, H * i : H * (i + 1)]
    sym_q[...] = jnp.zeros_like(sym_q)
    for k in range(HALF):
        pairs_from(full, k, FP, sym_q)
    sym_q[pl.ds(FP * HALF, F), :] = full[pl.ds(F, F, stride=FP), :]
    sym_q[pl.ds(FP * HALF + F, 1), :] = out_w[0:1, :]
    a_ref[:, :H] = sym_w[:PAIRS].astype(BF)
    a_ref[:, H:] = sym_q[:PAIRS].astype(BF)
    for b in range(PL // 128):
        at_ref[:H, 128 * b : 128 * (b + 1)] = jnp.transpose(sym_w[128 * b : 128 * (b + 1)]).astype(BF)
        at_ref[H:, 128 * b : 128 * (b + 1)] = jnp.transpose(sym_q[128 * b : 128 * (b + 1)]).astype(BF)


def forward(x, at_ref, xx, z_ref, y_ref):
    xx[0:FP, :] = x
    xx[F : F + FP, :] = x
    ones = xx[0:FP, :]
    field = lax.broadcasted_iota(jnp.int32, (FP, LANES), 0)
    x1 = jnp.where(field == F, 1.0, ones)
    for b in range(HALF // 2):
        two = [x1 * xx[pl.ds(k, FP), :] for k in (2 * b, 2 * b + 1)]
        z_ref[pl.ds(2 * FP * b, 2 * FP), :] = jnp.concatenate(two, axis=0).astype(BF)
    z_ref[pl.ds(FP * HALF, PL - FP * HALF), :] = jnp.concatenate(
        [x1, jnp.zeros((PL - FP * HALF - FP, LANES), F32)], axis=0
    ).astype(BF)
    y_ref[...] = dot(at_ref[...], z_ref[...], 1, 0)
    total = jnp.sum(y_ref[:H, :] * y_ref[H:, :], axis=0, keepdims=True)
    total = jnp.concatenate([total[:, 128 * t : 128 * (t + 1)] for t in range(T2N)], axis=0)
    total = jnp.concatenate(
        [total[2 * t : 2 * t + 1] + total[2 * t + 1 : 2 * t + 2] for t in range(T2D)], axis=0
    )
    first = lax.broadcasted_iota(jnp.int32, total.shape, 1) < 64
    low = jnp.sum(jnp.where(first, total, 0.0), axis=1, keepdims=True)
    high = jnp.sum(jnp.where(first, 0.0, total), axis=1, keepdims=True)
    return jnp.where(first, low, high)


def slope_row(logits, labels_ref, first):
    row = lax.broadcasted_iota(jnp.int32, logits.shape, 0)
    lane = lax.broadcasted_iota(jnp.int32, logits.shape, 1)
    sample = 2 * row + (lane >= 64).astype(jnp.int32)
    labels = jnp.zeros(logits.shape, F32)
    for n in range(2 * T2D):
        labels = jnp.where(sample == n, labels_ref[first + n].astype(F32), labels)
    slope = SCALE * (1.0 / (1.0 + jnp.exp(-logits)) - labels)
    return jnp.concatenate([slope[t // 2 : t // 2 + 1] for t in range(T2N)], axis=1)


def field_grads(a_ref, y16, xx, acc):
    swapped = jnp.concatenate([y16[H:], y16[:H]], axis=0)
    r = dot(a_ref[...], swapped, 1, 0)
    field = lax.broadcasted_iota(jnp.int32, (FP, LANES), 0)
    acc[...] = jnp.zeros_like(acc)
    total = r[FP * HALF : FP * HALF + FP]
    x = xx[0:FP, :]
    for k in range(HALF):
        block = r[FP * k : FP * (k + 1)]
        total = total + block * xx[pl.ds(k, FP), :]
        acc[pl.ds(k, FP), :] += block * x
    total = total + acc[0:FP, :] + acc[F : F + FP, :]
    return jnp.where(field == F, 0.0, total)


def finish_first(sums, mine, full, g1_ref):
    for k in range(HALF):
        pairs_to(sums, PAIRS, k, F, full)
    g1_ref[...] = dot(mine, full[pl.ds(0, F * F), :].astype(BF), 1, 1)


def finish_rest(t2, u_mine, w3_mine, w2p_ref, full, tall, g2_ref, g3_ref):
    for k in range(HALF):
        pairs_to(t2, 0, k, FP, full)
    full[pl.ds(F, F, stride=FP), :] = t2[pl.ds(FP * HALF, F), :]
    wide = jnp.concatenate([full[pl.ds(FP * i, FP), :] for i in range(F)], axis=1).astype(BF)
    two = dot(u_mine[:, :FP], wide, 1, 0)
    v3 = dot(wide, w2p_ref[...], 1, 0)
    rows = []
    for i in range(F):
        rows.append(two[:, H * i : H * (i + 1)])
        rows.append(w3_mine * v3[i : i + 1])
    rows.append(jnp.zeros((16, 128), F32))
    lane = lax.broadcasted_iota(jnp.int32, (H, 128), 1) // 16
    for b in range(5):
        block = jnp.transpose(jnp.concatenate(rows[16 * b : 16 * (b + 1)], axis=0))
        for i in range(8 * b, min(8 * b + 8, F)):
            tall[pl.ds(i, H, stride=F), :] = jnp.where(lane == i - 8 * b, block, 0.0)
    row = lax.broadcasted_iota(jnp.int32, (16, 128), 0)
    pick = jnp.where(lax.broadcasted_iota(jnp.int32, (16, 128), 1) % 16 == row, 1.0, 0.0).astype(BF)
    out = dot(pick, tall[...].astype(BF), 1, 1)
    g2_ref[...] = out[:8]
    g3_ref[...] = out[8:]


MESH = pl.DeviceIdType.MESH
SUMROWS = 1664
CUTS = (0, 512, 1024, SUMROWS)


class Group:
    def __init__(self, n, me, device):
        self.n, self.me, self.device = n, me, device

    def others(self):
        return [lax.rem(self.me + r, self.n) for r in range(1, self.n)]

    def send(self, source, dst, sems):
        copies = []
        for r, p in enumerate(self.others()):
            copies.append(
                pltpu.make_async_remote_copy(
                    src_ref=source(p),
                    dst_ref=dst.at[self.me],
                    send_sem=sems.at[0, r],
                    recv_sem=sems.at[1, r],
                    device_id=self.device(p),
                    device_id_type=MESH,
                )
            )
            copies[-1].start()
        return copies


def arrived(copies):
    for c in copies:
        c.wait_recv()


def added(ref, n):
    total = ref[0].astype(F32)
    for p in range(1, n):
        total = total + ref[p].astype(F32)
    return total


def k_main(
    ids_in, rows_in, slots_in_ref, labels_in, ow_in, w1_in, w2_in, w3_in,
    rg, w2p, sums_ref, um_ref, mine_ref, w3m_ref,
    ids_ref, rows_ref, slots_ref, labels_ref, ow_ref, w1_ref, w2, w3, tall, full, sym_q, sym_w, u_ref,
    a_ref, at_ref, member, xx, z_ref, y_ref, acc,
    pooled, bags, slots_out, slots_in, chooser_ref, *rest,
):
    parts = [rest[5 * i : 5 * i + 5] for i in range(3)]
    sems = [rest[15 + 4 * i : 19 + 4 * i] for i in range(3)]
    load_sems, bag_sems, slot_sems = rest[27:]
    dp, samp, col = lax.axis_index("dp"), lax.axis_index("samp"), lax.axis_index("col")
    yy, xc = dp // 4, lax.rem(dp, 4)
    zz, core = col * 2 + samp // 2, lax.rem(samp, 2)
    q = samp * 2 + col

    def device(x=xc, y=yy, z=zz, c=core):
        return {"dp": y * 4 + x, "samp": lax.rem(z, 2) * 2 + c, "col": z // 2}

    column = Group(8, q, lambda p: {"dp": dp, "samp": p // 2, "col": lax.rem(p, 2)})
    x4 = Group(4, xc, lambda p: device(x=p))
    y4 = Group(4, yy, lambda p: device(y=p))
    z4 = Group(4, zz, lambda p: device(z=p))
    x8 = Group(8, xc * 2 + core, lambda p: device(x=p // 2, c=lax.rem(p, 2)))
    y8 = Group(8, yy * 2 + core, lambda p: device(y=p // 2, c=lax.rem(p, 2)))
    z8 = Group(8, zz * 2 + core, lambda p: device(z=p // 2, c=lax.rem(p, 2)))
    orders = ((z8, x4, y4), (x8, y4, z4), (y8, z4, x4))

    barrier = pltpu.get_barrier_semaphore()
    for p in column.others():
        pl.semaphore_signal(barrier, inc=1, device_id=column.device(p), device_id_type=MESH)
    for r in range(1, 4):
        for c in range(2):
            for peer in (device(x=lax.rem(xc + r, 4), c=c), device(y=lax.rem(yy + r, 4), c=c)):
                pl.semaphore_signal(barrier, inc=1, device_id=peer, device_id_type=MESH)
    loads = []
    for n, (source, target) in enumerate((
        (ids_in, ids_ref), (rows_in, rows_ref), (ow_in, ow_ref), (w3_in, w3), (w1_in, w1_ref), (w2_in, w2),
        (slots_in_ref, slots_ref), (labels_in, labels_ref),
    )):
        loads.append(pltpu.make_async_copy(source, target, load_sems.at[n]))
        loads[-1].start()
    loads[0].wait()
    loads[1].wait()

    ids = ids_ref[...]
    member[...] = bag_member(ids)
    pooled[...] = pool(ids, rows_ref[0], member[...]).reshape(8, CHUNK, 128)
    bags[q] = pooled[q]
    pl.semaphore_wait(barrier, 19)
    to_bags = column.send(lambda p: pooled.at[p], bags, bag_sems)
    for c in loads[2:]:
        c.wait()
    out_w = ow_ref[...].astype(F32)
    prepare_first(w1_ref, w3, out_w, tall, full, sym_w, u_ref)
    prepare_rest(w2, out_w, tall, full, sym_q, sym_w, u_ref, w2p, a_ref, at_ref)
    row = lax.broadcasted_iota(jnp.int32, (8, 128), 0)
    lane = lax.broadcasted_iota(jnp.int32, (8, 128), 1)
    mine = jnp.where(lane == row + 8 * dp, 1.0, 0.0)
    mine_ref[...] = mine
    um_ref[...] = dot(mine.astype(BF), u_ref[...], 1, 0)
    w3_mine = jnp.sum(mine * out_w[2:3, :], axis=1, keepdims=True)
    w3m_ref[...] = jnp.broadcast_to(w3_mine, (8, 128))

    chooser_ref[...] = field_chooser(slots_ref[...])
    arrived(to_bags)
    x = gather_fields(chooser_ref[...], bags[...].reshape(4, 2, CHUNK, 128))
    slope = slope_row(forward(x, at_ref, xx, z_ref, y_ref), labels_ref, 12 * col)
    both = dot(z_ref[...], (y_ref[...] * slope).astype(BF), 1, 1)
    flat = jnp.concatenate(
        [both[:PAIRS, :H], both[: FP * HALF, H:], jnp.zeros((SUMROWS - PAIRS - FP * HALF, 128), F32)], axis=0
    ).astype(BF)
    sent = list(to_bags)
    flying = []
    for i, (part, order) in enumerate(zip(parts, orders)):
        whole, landed = part[0], part[1]
        whole[...] = flat[CUTS[i] : CUTS[i + 1]].reshape(whole.shape)
        landed[order[0].me] = whole[order[0].me]
        flying.append(order[0].send(lambda p, whole=whole: whole.at[p], landed, sems[i][0]))
    grads = field_grads(a_ref, y_ref[...].astype(BF), xx, acc) * slope
    halves = scatter_fields(slots_ref[...], grads)
    for owner in range(4):
        for h in range(2):
            slots_out[2 * owner + h] = halves[h][CHUNK * owner : CHUNK * (owner + 1)]
    slots_in[q] = slots_out[q]
    to_slots = column.send(lambda p: slots_out.at[p], slots_in, slot_sems)
    sent = sent + to_slots

    for stage in range(1, 4):
        if stage == 3:
            arrived(to_slots)
        for i, (part, order) in enumerate(zip(parts, orders)):
            arrived(flying[i])
            sent = sent + flying[i]
            group = order[stage] if stage < 3 else order[0]
            source, landed = part[stage], part[stage + 1]
            landed[group.me] = added(source, 8 if stage == 1 else 4).astype(BF)
            flying[i] = group.send(lambda p, landed=landed, me=group.me: landed.at[me], landed, sems[i][stage])
    rg[0] = spread_rows(ids, member[...], slots_in[...].reshape(BAGS, 128))
    for i, part in enumerate(parts):
        arrived(flying[i])
        sent = sent + flying[i]
        sums_ref[pl.ds(CUTS[i], CUTS[i + 1] - CUTS[i]), :] = part[4][...].reshape(CUTS[i + 1] - CUTS[i], 128)
    for c in sent:
        c.wait_send()


def shape(dims, dtype):
    return jax.ShapeDtypeStruct(dims, dtype)


TALL = pltpu.VMEM((F * H, 128), F32)
FULL = pltpu.VMEM((F * FP, 128), F32)
ANY = pl.BlockSpec(memory_space=pl.ANY)


def pair_sems(n):
    return pltpu.SemaphoreType.DMA((2, n - 1))


def run_main(ids, rows, slots, labels, ow, w1, w2, w3):
    n = ids.shape[1]
    vm = pltpu.VMEM
    sym = vm((PL, 128), F32)
    scratch = [
        vm(ids.shape, jnp.int32), vm(rows.shape, BF), vm(slots.shape, jnp.int32), pltpu.SMEM(labels.shape, jnp.int32),
        vm(ow.shape, BF), vm(w1.shape, BF), vm((H, F * H), BF), vm((H, F * H), BF), TALL, FULL, sym, sym, vm((H, 128), BF),
        vm((PAIRS, 256), BF), vm((256, PL), BF), vm((BAGS, n), BF),
        vm((88, LANES), F32), vm((PL, LANES), BF), vm((256, LANES), F32), vm((88, LANES), F32),
        vm((8, CHUNK, 128), BF), vm((8, CHUNK, 128), BF), vm((8, CHUNK, 128), BF), vm((8, CHUNK, 128), BF),
        vm((FP * T2D, 256), BF),
    ]
    for low, high in zip(CUTS, CUTS[1:]):
        scratch += [vm((k, (high - low) // 8, 128), BF) for k in (8, 8, 4, 4, 8)]
    scratch += [pair_sems(k) for _ in range(3) for k in (8, 4, 4, 8)]
    scratch += [pltpu.SemaphoreType.DMA((8,)), pair_sems(8), pair_sems(8)]
    return pl.pallas_call(
        k_main,
        out_shape=[
            vm((1, 64, n), BF), vm((F * H, 128), BF), vm((SUMROWS, 128), BF),
            vm((8, 128), F32), vm((8, 128), F32), vm((8, 128), F32),
        ],
        in_specs=[ANY] * 8,
        out_specs=[VMEM] * 6,
        scratch_shapes=scratch,
        compiler_params=pltpu.CompilerParams(collective_id=0, has_side_effects=True, vmem_limit_bytes=53 << 20),
    )(ids, rows, slots, labels, ow, w1, w2, w3)


def k_finish(rows_in, w2p, sums_in, um_ref, mine_ref, w3m_ref, rg_ref, g1_ref, g2_ref, g3_ref, full, tall, sums):
    rg_ref[...] = rows_in[...]
    sums[...] = sums_in[...].astype(F32)
    finish_first(sums, mine_ref[...].astype(BF), full, g1_ref)
    finish_rest(sums, um_ref[...].astype(BF), w3m_ref[...], w2p, full, tall, g2_ref, g3_ref)


def run_finish(rows, w2p, sums, um, mine, w3m):
    return pl.pallas_call(
        k_finish,
        out_shape=[
            shape(rows.shape, BF), shape((8, F * F), F32), shape((8, F * H), F32), shape((8, F * H), F32)
        ],
        in_specs=[VMEM] * 6,
        out_specs=[VMEM] * 4,
        scratch_shapes=[FULL, TALL, pltpu.VMEM(sums.shape, F32)],
        compiler_params=pltpu.CompilerParams(vmem_limit_bytes=30 << 20),
    )(rows, w2p, sums, um, mine, w3m)


def local(looked_rows, bag_ids, slot_of, labels, out_weight, filter_first, filter_second, filter_third):
    parts = run_main(
        bag_ids, jnp.swapaxes(looked_rows, 1, 2), slot_of.reshape(1, FP), labels, out_weight,
        filter_first.T, filter_second, filter_third,
    )
    rows, first, second, third = run_finish(*parts)
    return jnp.swapaxes(rows, 1, 2), first, second, third


def solution(mesh):
    in_specs = (
        P(("dp", "samp"), None, "col"),
        P(("dp", "samp"), None),
        P(),
        P(("dp", "samp")),
        P(),
        P(),
        P(),
        P(),
    )
    out_specs = (P(("dp", "samp"), None, "col"), P("dp", None), P("dp", None), P("dp", None))
    return jax.shard_map(local, mesh=mesh, in_specs=in_specs, out_specs=out_specs, check_vma=False)
```

```python
import functools

import jax
import jax.numpy as jnp
from jax import lax
from jax.experimental import pallas as pl
from jax.experimental.pallas import tpu as pltpu
from jax.sharding import PartitionSpec as P

F = 39
FP = 40
H = 128
HALF = 20
PAIRS = 848
PL = 896
LANES = 1536
T2N = 12
BAGS = 512
CHUNK = 64
T2D = 6
SCALE = 16.0
BF = jnp.bfloat16
F32 = jnp.float32
VMEM = pl.BlockSpec(memory_space=pltpu.VMEM)
SMEM = pl.BlockSpec(memory_space=pltpu.SMEM)


def dot(a, b, ca, cb):
    return lax.dot_general(a, b, (((ca,), (cb,)), ((), ())), preferred_element_type=F32)


def lane_columns(row):
    n = row.shape[1] // 128
    blocks = [
        jnp.transpose(jnp.broadcast_to(row[:, b * 128 : (b + 1) * 128], (128, 128)))
        for b in range(n)
    ]
    return jnp.concatenate(blocks, axis=0)


def bag_places(ids):
    tens = (ids * 6554) >> 16
    twenties = (ids * 3277) >> 16
    row = twenties * 10 + (ids - tens * 10)
    row = row + 4 * ((row * 17477) >> 20)
    return row, tens - 2 * twenties


def bag_member(ids):
    place, _ = bag_places(ids)
    n = ids.shape[1]
    spot = lax.broadcasted_iota(jnp.int32, (BAGS, n), 0)
    return jnp.where(jnp.broadcast_to(place, (BAGS, n)) == spot, 1.0, 0.0).astype(BF)


def pool(ids, rows, member):
    half = bag_places(ids)[1].astype(F32)
    rows = rows.astype(F32)
    wide = jnp.concatenate([rows * (1.0 - half), rows * half], axis=0).astype(BF)
    return dot(member, wide, 1, 1).astype(BF)


def slot_row(slots):
    owner = (slots * 6554) >> 16
    base = owner * CHUNK + (slots - owner * 10)
    parts = [base + 10 * t for t in range(T2D)]
    parts.append(jnp.full((1, 256 - FP * T2D), -1, jnp.int32))
    return jnp.concatenate(parts, axis=1)


def field_chooser(slots):
    col = lane_columns(slot_row(slots).astype(F32))[: FP * T2D]
    parts = []
    for b in range(2):
        lane = lax.broadcasted_iota(jnp.int32, col.shape, 1) + 128 * b
        parts.append(jnp.where(col == lane.astype(F32), 1.0, 0.0).astype(BF))
    return jnp.concatenate(parts, axis=1)


def gather_fields(chooser, bags):
    wide = jnp.concatenate([bags[:, h].reshape(4 * CHUNK, 128) for h in range(2)], axis=1)
    picked = dot(chooser, wide, 1, 0)
    x = jnp.concatenate([picked[FP * t : FP * (t + 1)] for t in range(T2D)], axis=1)
    field = lax.broadcasted_iota(jnp.int32, x.shape, 0)
    return jnp.where(field == F, 1.0, x)


def scatter_fields(slots, grads):
    row = slot_row(slots)
    spot = lax.broadcasted_iota(jnp.int32, (4 * CHUNK, 256), 0)
    member = jnp.where(jnp.broadcast_to(row, (4 * CHUNK, 256)) == spot, 1.0, 0.0).astype(BF)
    tall = [grads[:, 256 * t : 256 * (t + 1)] for t in range(T2D)]
    tall.append(jnp.zeros((256 - FP * T2D, 256), F32))
    both = dot(member, jnp.concatenate(tall, axis=0).astype(BF), 1, 0).astype(BF)
    return both[:, :128], both[:, 128:]


def spread_rows(ids, member, returned):
    half = bag_places(ids)[1]
    both = dot(returned, member, 0, 0)
    return jnp.where(half == 0, both[:64], both[64:]).astype(BF)


def pairs_from(full, k, stride, out, zero_tail=True):
    step = stride + 1
    low = full[pl.ds(k, F - k, stride=step), :]
    if k:
        low = low + full[pl.ds(k * stride, F - k, stride=step), :]
    out[pl.ds(FP * k, F - k), :] = low
    if k:
        high = full[pl.ds((F - k) * stride, k, stride=step), :]
        high = high + full[pl.ds(F - k, k, stride=step), :]
        out[pl.ds(FP * k + F - k, k), :] = high


def pairs_to(src, first, k, stride, full):
    step = stride + 1
    low = src[pl.ds(first + FP * k, F - k), :]
    full[pl.ds(k, F - k, stride=step), :] = low
    if k:
        full[pl.ds(k * stride, F - k, stride=step), :] = low
        high = src[pl.ds(first + FP * k + F - k, k), :]
        full[pl.ds((F - k) * stride, k, stride=step), :] = high
        full[pl.ds(F - k, k, stride=step), :] = high


def prepare_first(w1_ref, w3_ref, out_w, tall, full, sym_w, u_ref):
    lane = lax.broadcasted_iota(jnp.int32, (H, 128), 1)
    w3_col = lane_columns(out_w[2:3, :]).astype(BF)
    tall[...] = dot(w3_ref[...], w3_col, 0, 0)
    u = jnp.where(lane == F, lane_columns(out_w[1:2, :]), 0.0)
    for i in range(F):
        u = jnp.where(lane == i, tall[pl.ds(i, H, stride=F), :], u)
    u = u.astype(BF)
    u_ref[...] = u
    full[pl.ds(0, F * F), :] = w1_ref[...].astype(F32)
    sym_w[...] = jnp.zeros_like(sym_w)
    for k in range(HALF):
        pairs_from(full, k, F, sym_w)


def prepare_rest(w2_ref, out_w, tall, full, sym_q, sym_w, u_ref, w2p_ref, a_ref, at_ref):
    lane = lax.broadcasted_iota(jnp.int32, (H, 128), 1)
    sublane = lax.broadcasted_iota(jnp.int32, (H, 128), 0)
    tall[...] = dot(w2_ref[...], jnp.where(lane == sublane, 1.0, 0.0).astype(BF), 0, 0)
    for i in range(F):
        w2p_ref[pl.ds(H * i, H), :] = tall[pl.ds(i, H, stride=F), :].astype(BF)
    turned = jnp.transpose(u_ref[...].astype(F32))[:FP].astype(BF)
    blocks = dot(turned, w2p_ref[...], 1, 1)
    for i in range(F):
        full[pl.ds(FP * i, FP), :] = blocks[:, H * i : H * (i + 1)]
    sym_q[...] = jnp.zeros_like(sym_q)
    for k in range(HALF):
        pairs_from(full, k, FP, sym_q)
    sym_q[pl.ds(FP * HALF, F), :] = full[pl.ds(F, F, stride=FP), :]
    sym_q[pl.ds(FP * HALF + F, 1), :] = out_w[0:1, :]
    a_ref[:, :H] = sym_w[:PAIRS].astype(BF)
    a_ref[:, H:] = sym_q[:PAIRS].astype(BF)
    for b in range(PL // 128):
        at_ref[:H, 128 * b : 128 * (b + 1)] = jnp.transpose(sym_w[128 * b : 128 * (b + 1)]).astype(BF)
        at_ref[H:, 128 * b : 128 * (b + 1)] = jnp.transpose(sym_q[128 * b : 128 * (b + 1)]).astype(BF)


def forward(x, at_ref, xx, z_ref, y_ref):
    xx[0:FP, :] = x
    xx[F : F + FP, :] = x
    ones = xx[0:FP, :]
    field = lax.broadcasted_iota(jnp.int32, (FP, LANES), 0)
    x1 = jnp.where(field == F, 1.0, ones)
    for b in range(HALF // 2):
        two = [x1 * xx[pl.ds(k, FP), :] for k in (2 * b, 2 * b + 1)]
        z_ref[pl.ds(2 * FP * b, 2 * FP), :] = jnp.concatenate(two, axis=0).astype(BF)
    z_ref[pl.ds(FP * HALF, PL - FP * HALF), :] = jnp.concatenate(
        [x1, jnp.zeros((PL - FP * HALF - FP, LANES), F32)], axis=0
    ).astype(BF)
    y_ref[...] = dot(at_ref[...], z_ref[...], 1, 0)
    total = jnp.sum(y_ref[:H, :] * y_ref[H:, :], axis=0, keepdims=True)
    total = jnp.concatenate([total[:, 128 * t : 128 * (t + 1)] for t in range(T2N)], axis=0)
    total = jnp.concatenate(
        [total[2 * t : 2 * t + 1] + total[2 * t + 1 : 2 * t + 2] for t in range(T2D)], axis=0
    )
    first = lax.broadcasted_iota(jnp.int32, total.shape, 1) < 64
    low = jnp.sum(jnp.where(first, total, 0.0), axis=1, keepdims=True)
    high = jnp.sum(jnp.where(first, 0.0, total), axis=1, keepdims=True)
    return jnp.where(first, low, high)


def slope_row(logits, labels_ref, first):
    row = lax.broadcasted_iota(jnp.int32, logits.shape, 0)
    lane = lax.broadcasted_iota(jnp.int32, logits.shape, 1)
    sample = 2 * row + (lane >= 64).astype(jnp.int32)
    labels = jnp.zeros(logits.shape, F32)
    for n in range(2 * T2D):
        labels = jnp.where(sample == n, labels_ref[first + n].astype(F32), labels)
    slope = SCALE * (1.0 / (1.0 + jnp.exp(-logits)) - labels)
    return jnp.concatenate([slope[t // 2 : t // 2 + 1] for t in range(T2N)], axis=1)


def field_grads(a_ref, y16, xx, acc):
    swapped = jnp.concatenate([y16[H:], y16[:H]], axis=0)
    r = dot(a_ref[...], swapped, 1, 0)
    field = lax.broadcasted_iota(jnp.int32, (FP, LANES), 0)
    acc[...] = jnp.zeros_like(acc)
    total = r[FP * HALF : FP * HALF + FP]
    x = xx[0:FP, :]
    for k in range(HALF):
        block = r[FP * k : FP * (k + 1)]
        total = total + block * xx[pl.ds(k, FP), :]
        acc[pl.ds(k, FP), :] += block * x
    total = total + acc[0:FP, :] + acc[F : F + FP, :]
    return jnp.where(field == F, 0.0, total)


def finish_first(sums, mine, full, g1_ref):
    for k in range(HALF):
        pairs_to(sums, PAIRS, k, F, full)
    g1_ref[...] = dot(mine, full[pl.ds(0, F * F), :].astype(BF), 1, 1)


def finish_rest(t2, u_mine, w3_mine, w2p_ref, full, tall, g2_ref, g3_ref):
    for k in range(HALF):
        pairs_to(t2, 0, k, FP, full)
    full[pl.ds(F, F, stride=FP), :] = t2[pl.ds(FP * HALF, F), :]
    wide = jnp.concatenate([full[pl.ds(FP * i, FP), :] for i in range(F)], axis=1).astype(BF)
    two = dot(u_mine[:, :FP], wide, 1, 0)
    v3 = dot(wide, w2p_ref[...], 1, 0)
    rows = []
    for i in range(F):
        rows.append(two[:, H * i : H * (i + 1)])
        rows.append(w3_mine * v3[i : i + 1])
    rows.append(jnp.zeros((16, 128), F32))
    lane = lax.broadcasted_iota(jnp.int32, (H, 128), 1) // 16
    for b in range(5):
        block = jnp.transpose(jnp.concatenate(rows[16 * b : 16 * (b + 1)], axis=0))
        for i in range(8 * b, min(8 * b + 8, F)):
            tall[pl.ds(i, H, stride=F), :] = jnp.where(lane == i - 8 * b, block, 0.0)
    row = lax.broadcasted_iota(jnp.int32, (16, 128), 0)
    pick = jnp.where(lax.broadcasted_iota(jnp.int32, (16, 128), 1) % 16 == row, 1.0, 0.0).astype(BF)
    out = dot(pick, tall[...].astype(BF), 1, 1)
    g2_ref[...] = out[:8]
    g3_ref[...] = out[8:]


MESH = pl.DeviceIdType.MESH
SUMROWS = 1664
ZCUTS = (0, 256, 512, PAIRS)
CUTS = (0, 512, 1024, SUMROWS)


class Group:
    def __init__(self, n, me, device):
        self.n, self.me, self.device = n, me, device

    def others(self):
        return [lax.rem(self.me + r, self.n) for r in range(1, self.n)]

    def send(self, source, dst, sems):
        copies = []
        for r, p in enumerate(self.others()):
            copies.append(
                pltpu.make_async_remote_copy(
                    src_ref=source(p),
                    dst_ref=dst.at[self.me],
                    send_sem=sems.at[0, r],
                    recv_sem=sems.at[1, r],
                    device_id=self.device(p),
                    device_id_type=MESH,
                )
            )
            copies[-1].start()
        return copies


def arrived(copies):
    for c in copies:
        c.wait_recv()


def added(ref, n):
    total = ref[0].astype(F32)
    for p in range(1, n):
        total = total + ref[p].astype(F32)
    return total


def k_main(
    ids_in, rows_in, slots_in_ref, labels_in, ow_in, w1_in, w2_in, w3_in,
    rg, w2p, sums_ref, um_ref, mine_ref, w3m_ref,
    ids_ref, rows_ref, slots_ref, labels_ref, ow_ref, w1_ref, w2, w3, tall, full, sym_q, sym_w, u_ref,
    a_ref, at_ref, member, xx, z_ref, y_ref, acc,
    pooled, bags, slots_out, slots_in, chooser_ref, *rest,
):
    parts = [rest[5 * i : 5 * i + 5] for i in range(3)]
    sems = [rest[15 + 4 * i : 19 + 4 * i] for i in range(3)]
    load_sems, bag_sems, slot_sems = rest[27:]
    dp, samp, col = lax.axis_index("dp"), lax.axis_index("samp"), lax.axis_index("col")
    yy, xc = dp // 4, lax.rem(dp, 4)
    zz, core = col * 2 + samp // 2, lax.rem(samp, 2)
    q = samp * 2 + col

    def device(x=xc, y=yy, z=zz, c=core):
        return {"dp": y * 4 + x, "samp": lax.rem(z, 2) * 2 + c, "col": z // 2}

    column = Group(8, q, lambda p: {"dp": dp, "samp": p // 2, "col": lax.rem(p, 2)})
    x4 = Group(4, xc, lambda p: device(x=p))
    y4 = Group(4, yy, lambda p: device(y=p))
    z4 = Group(4, zz, lambda p: device(z=p))
    x8 = Group(8, xc * 2 + core, lambda p: device(x=p // 2, c=lax.rem(p, 2)))
    y8 = Group(8, yy * 2 + core, lambda p: device(y=p // 2, c=lax.rem(p, 2)))
    z8 = Group(8, zz * 2 + core, lambda p: device(z=p // 2, c=lax.rem(p, 2)))
    orders = ((z8, x4, y4), (x8, y4, z4), (y8, z4, x4))

    loads = []
    for n, (source, target) in enumerate((
        (ids_in, ids_ref), (rows_in, rows_ref), (ow_in, ow_ref), (w3_in, w3), (w1_in, w1_ref), (w2_in, w2),
        (slots_in_ref, slots_ref), (labels_in, labels_ref),
    )):
        loads.append(pltpu.make_async_copy(source, target, load_sems.at[n]))
    for c in loads[:2]:
        c.start()
    barrier = pltpu.get_barrier_semaphore()
    for p in column.others():
        pl.semaphore_signal(barrier, inc=1, device_id=column.device(p), device_id_type=MESH)
    for r in range(1, 4):
        for c in range(2):
            for peer in (device(x=lax.rem(xc + r, 4), c=c), device(y=lax.rem(yy + r, 4), c=c)):
                pl.semaphore_signal(barrier, inc=1, device_id=peer, device_id_type=MESH)
    for c in loads[2:]:
        c.start()
    loads[0].wait()
    loads[1].wait()

    ids = ids_ref[...]
    member[...] = bag_member(ids)
    pooled[...] = pool(ids, rows_ref[0], member[...]).reshape(8, CHUNK, 128)
    bags[q] = pooled[q]
    pl.semaphore_wait(barrier, 19)
    to_bags = column.send(lambda p: pooled.at[p], bags, bag_sems)
    for c in loads[2:]:
        c.wait()
    out_w = ow_ref[...].astype(F32)
    prepare_first(w1_ref, w3, out_w, tall, full, sym_w, u_ref)
    prepare_rest(w2, out_w, tall, full, sym_q, sym_w, u_ref, w2p, a_ref, at_ref)
    row = lax.broadcasted_iota(jnp.int32, (8, 128), 0)
    lane = lax.broadcasted_iota(jnp.int32, (8, 128), 1)
    mine = jnp.where(lane == row + 8 * dp, 1.0, 0.0)
    mine_ref[...] = mine
    um_ref[...] = dot(mine.astype(BF), u_ref[...], 1, 0)
    w3_mine = jnp.sum(mine * out_w[2:3, :], axis=1, keepdims=True)
    w3m_ref[...] = jnp.broadcast_to(w3_mine, (8, 128))

    chooser_ref[...] = field_chooser(slots_ref[...])
    arrived(to_bags)
    x = gather_fields(chooser_ref[...], bags[...].reshape(4, 2, CHUNK, 128))
    slope = slope_row(forward(x, at_ref, xx, z_ref, y_ref), labels_ref, 12 * col)
    scaled = (y_ref[...] * slope).astype(BF)
    sent = list(to_bags)
    flying = []
    for i, (part, order) in enumerate(zip(parts, orders)):
        whole, landed = part[0], part[1]
        low, high = ZCUTS[i], ZCUTS[i + 1]
        both = dot(z_ref[low:high], scaled, 1, 1)
        rows = [both[:, :H], both[: min(high, FP * HALF) - low, H:]]
        left = CUTS[i + 1] - CUTS[i] - sum(r.shape[0] for r in rows)
        if left:
            rows.append(jnp.zeros((left, 128), F32))
        whole[...] = jnp.concatenate(rows, axis=0).astype(BF).reshape(whole.shape)
        landed[order[0].me] = whole[order[0].me]
        flying.append(order[0].send(lambda p, whole=whole: whole.at[p], landed, sems[i][0]))
    grads = field_grads(a_ref, y_ref[...].astype(BF), xx, acc) * slope
    halves = scatter_fields(slots_ref[...], grads)
    for owner in range(4):
        for h in range(2):
            slots_out[2 * owner + h] = halves[h][CHUNK * owner : CHUNK * (owner + 1)]
    slots_in[q] = slots_out[q]
    to_slots = column.send(lambda p: slots_out.at[p], slots_in, slot_sems)
    sent = sent + to_slots

    for stage in range(1, 4):
        if stage == 3:
            arrived(to_slots)
        for i, (part, order) in enumerate(zip(parts, orders)):
            arrived(flying[i])
            sent = sent + flying[i]
            group = order[stage] if stage < 3 else order[0]
            source, landed = part[stage], part[stage + 1]
            landed[group.me] = added(source, 8 if stage == 1 else 4).astype(BF)
            flying[i] = group.send(lambda p, landed=landed, me=group.me: landed.at[me], landed, sems[i][stage])
    rg[0] = spread_rows(ids, member[...], slots_in[...].reshape(BAGS, 128))
    for i, part in enumerate(parts):
        arrived(flying[i])
        sent = sent + flying[i]
        sums_ref[pl.ds(CUTS[i], CUTS[i + 1] - CUTS[i]), :] = part[4][...].reshape(CUTS[i + 1] - CUTS[i], 128)
    for c in sent:
        c.wait_send()


def shape(dims, dtype):
    return jax.ShapeDtypeStruct(dims, dtype)


TALL = pltpu.VMEM((F * H, 128), F32)
FULL = pltpu.VMEM((F * FP, 128), F32)
ANY = pl.BlockSpec(memory_space=pl.ANY)


def pair_sems(n):
    return pltpu.SemaphoreType.DMA((2, n - 1))


def run_main(ids, rows, slots, labels, ow, w1, w2, w3):
    n = ids.shape[1]
    vm = pltpu.VMEM
    sym = vm((PL, 128), F32)
    scratch = [
        vm(ids.shape, jnp.int32), vm(rows.shape, BF), vm(slots.shape, jnp.int32), pltpu.SMEM(labels.shape, jnp.int32),
        vm(ow.shape, BF), vm(w1.shape, BF), vm((H, F * H), BF), vm((H, F * H), BF), TALL, FULL, sym, sym, vm((H, 128), BF),
        vm((PAIRS, 256), BF), vm((256, PL), BF), vm((BAGS, n), BF),
        vm((88, LANES), F32), vm((PL, LANES), BF), vm((256, LANES), F32), vm((88, LANES), F32),
        vm((8, CHUNK, 128), BF), vm((8, CHUNK, 128), BF), vm((8, CHUNK, 128), BF), vm((8, CHUNK, 128), BF),
        vm((FP * T2D, 256), BF),
    ]
    for low, high in zip(CUTS, CUTS[1:]):
        scratch += [vm((k, (high - low) // 8, 128), BF) for k in (8, 8, 4, 4, 8)]
    scratch += [pair_sems(k) for _ in range(3) for k in (8, 4, 4, 8)]
    scratch += [pltpu.SemaphoreType.DMA((8,)), pair_sems(8), pair_sems(8)]
    return pl.pallas_call(
        k_main,
        out_shape=[
            vm((1, 64, n), BF), vm((F * H, 128), BF), vm((SUMROWS, 128), BF),
            vm((8, 128), F32), vm((8, 128), F32), vm((8, 128), F32),
        ],
        in_specs=[ANY] * 8,
        out_specs=[VMEM] * 6,
        scratch_shapes=scratch,
        compiler_params=pltpu.CompilerParams(collective_id=0, has_side_effects=True, vmem_limit_bytes=53 << 20),
    )(ids, rows, slots, labels, ow, w1, w2, w3)


def k_finish(rows_in, w2p, sums_in, um_ref, mine_ref, w3m_ref, rg_out, g1_ref, g2_ref, g3_ref, full, tall, sums, sem):
    rows = pltpu.make_async_copy(rows_in, rg_out, sem)
    rows.start()
    for i in range(3):
        low, high = ZCUTS[i], ZCUTS[i + 1]
        top = min(high, FP * HALF)
        sums[low:high, :] = sums_in[CUTS[i] : CUTS[i] + high - low, :].astype(F32)
        first = CUTS[i] + high - low
        sums[PAIRS + low : PAIRS + top, :] = sums_in[first : first + top - low, :].astype(F32)
    finish_first(sums, mine_ref[...].astype(BF), full, g1_ref)
    finish_rest(sums, um_ref[...].astype(BF), w3m_ref[...], w2p, full, tall, g2_ref, g3_ref)
    rows.wait()


def run_finish(rows, w2p, sums, um, mine, w3m):
    return pl.pallas_call(
        k_finish,
        out_shape=[
            shape(rows.shape, BF), shape((8, F * F), F32), shape((8, F * H), F32), shape((8, F * H), F32)
        ],
        in_specs=[VMEM] * 6,
        out_specs=[ANY] + [VMEM] * 3,
        scratch_shapes=[FULL, TALL, pltpu.VMEM(sums.shape, F32), pltpu.SemaphoreType.DMA(())],
        compiler_params=pltpu.CompilerParams(vmem_limit_bytes=30 << 20),
    )(rows, w2p, sums, um, mine, w3m)


def local(looked_rows, bag_ids, slot_of, labels, out_weight, filter_first, filter_second, filter_third):
    parts = run_main(
        bag_ids, jnp.swapaxes(looked_rows, 1, 2), slot_of.reshape(1, FP), labels, out_weight,
        filter_first.T, filter_second, filter_third,
    )
    rows, first, second, third = run_finish(*parts)
    return jnp.swapaxes(rows, 1, 2), first, second, third


def solution(mesh):
    in_specs = (
        P(("dp", "samp"), None, "col"),
        P(("dp", "samp"), None),
        P(),
        P(("dp", "samp")),
        P(),
        P(),
        P(),
        P(),
    )
    out_specs = (P(("dp", "samp"), None, "col"), P("dp", None), P("dp", None), P("dp", None))
    return jax.shard_map(local, mesh=mesh, in_specs=in_specs, out_specs=out_specs, check_vma=False)
```
